256 devices in a mesh: dp: 32 (over x_lo, z, core), tensor: 8 (over x_hi, y).
Axes of the slice: x: 4 (x_hi: 2, x_lo: 2; x = x_hi * 2 + x_lo), y: 4, z: 8, core: 2. Of those that a mesh axis runs over, the one named last changes fastest.
Arguments:
- hidden_acts: bfloat16 [256, 256, 14336], P('dp', None, 'tensor'), may hold values from -6 to 6
- out_grads: bfloat16 [256, 256, 4096], P('dp', None, 'tensor'), may hold values from -6 to 6
- input_basis: bfloat16 [64, 14336], P(None, 'tensor'), may hold values from -0.046875 to 0.046875
- output_basis: bfloat16 [64, 4096], P(None, 'tensor'), may hold values from -0.09375 to 0.09375
Outputs:
- gram_block: float32 [256, 256], P('dp', 'tensor')
The draws below stay inside these ranges and needn't reach their ends.
All inputs are finite; a program needn't handle non-finite values.
Results may differ from the reference program's by a relative error of at most 0.0003.
Values sent between devices are 32-bit elements; how exact they have to be, the bound alone decides.
A program may use at most 64 MiB of HBM per device.

```python
import math
import jax
import jax.numpy as jnp
from jax import lax

D = 4096
FF = 14336
K = 64
L = 256
SEQS = 256


def level_of(rng, shape, pieces, least, high):
    gain = 1.0
    for axis_at, parts in pieces:
        draws = jax.random.uniform(jax.random.fold_in(jax.random.fold_in(rng, 6), axis_at), (parts,), jnp.float32, least / len(pieces), high / len(pieces))
        gain = gain * jnp.repeat(jnp.exp(draws), shape[axis_at] // parts).reshape((-1,) + (1,) * (len(shape) - 1 - axis_at))
    return gain


def gaussian(own_key, shape, deviation, bound, pieces=(), kind=jnp.bfloat16):
    level = level_of(own_key, shape, pieces, -0.22, 0.18) if pieces else 1.0
    entries = jax.random.normal(own_key, shape, jnp.float32) * deviation * level
    return jnp.minimum(jnp.maximum(entries, -bound), bound).astype(kind)


def setup_inputs(seed: int = 0) -> dict:
    key_list = jax.random.split(jax.random.key(seed), 5)
    return {
        "hidden_acts": gaussian(key_list[0], (SEQS, L, FF), 1.0, 6.0, ((0, 32), (2, 8))),
        "out_grads": gaussian(key_list[1], (SEQS, L, D), 1.0, 6.0, ((0, 32), (2, 8))),
        "input_basis": gaussian(key_list[2], (K, FF), FF ** -0.5, 0.046875, ((1, 8),)),
        "output_basis": gaussian(key_list[3], (K, D), D ** -0.5, 0.09375, ((1, 8),)),
    }


def reference(hidden_acts, out_grads, input_basis, output_basis):
    left = jnp.dot(hidden_acts.reshape(-1, FF), input_basis.T, preferred_element_type=jnp.float32).reshape(SEQS, L, K)
    right = jnp.dot(out_grads.reshape(-1, D), output_basis.T, preferred_element_type=jnp.float32).reshape(SEQS, L, K)
    feats = jnp.einsum('sli,slj->sij', left, right, precision=lax.Precision.HIGHEST) * (1.0 / math.sqrt(L * K))
    feats = feats.reshape(SEQS, K * K)
    return jnp.dot(feats, feats.T, precision=lax.Precision.HIGHEST)
```

```python
import math

import jax
import jax.numpy as jnp
from jax import lax
from jax.experimental import pallas as pl
from jax.experimental.pallas import tpu as pltpu
from jax.sharding import PartitionSpec as P

MESH = pl.DeviceIdType.MESH
HIGHEST = lax.Precision.HIGHEST
NT = 8
NQ = 4
NZ = 8


def device(xl, z, c, xh, y):
    return {"dp": xl * 16 + z * 2 + c, "tensor": xh * 4 + y}


def contract_last(a, b, precision=None):
    return lax.dot_general(
        a, b, (((1,), (1,)), ((), ())), precision=precision, preferred_element_type=jnp.float32
    )


def kernel(
    h_hbm, o_hbm, pin_hbm, pout_hbm, out_ref,
    hbuf, obuf, wl, wr, part, recv, fbuf, ebuf, rows, cols, tiles, tiles_in,
    hsem, osem, wsem, rs_send, rs_recv, e_send, e_recv, row_send, row_recv, col_send, col_recv, t_send, t_recv,
):
    dp, me = lax.axis_index("dp"), lax.axis_index("tensor")
    xl, z, c = dp // 16, (dp // 2) % 8, dp % 2
    xh, y = me // 4, me % 4
    q = xl * 2 + c
    zpar, zrow = z % 2, z // 2

    win = pltpu.make_async_copy(pin_hbm, wl.at[pl.ds(0, 64)], wsem.at[0])
    wout = pltpu.make_async_copy(pout_hbm, wr.at[pl.ds(64, 64)], wsem.at[1])
    win.start()
    wout.start()

    def peer(off):
        return lax.rem(xh + off // 4, 2) * 4 + lax.rem(y + off % 4, 4)

    def load(off):
        s = peer(off)
        return (
            pltpu.make_async_copy(h_hbm.at[s], hbuf.at[off], hsem.at[off]),
            pltpu.make_async_copy(o_hbm.at[s], obuf.at[off], osem.at[off]),
        )

    for off in range(NT - 1, -1, -1):
        for copy in load(off):
            copy.start()

    barrier = pltpu.get_barrier_semaphore()

    def greet(dev):
        pl.semaphore_signal(barrier, inc=1, device_id=dev, device_id_type=MESH)

    for off in range(1, NT):
        t = peer(off)
        greet(device(xl, z, c, t // 4, t % 4))
    for j in range(1, NQ):
        p = q ^ j
        greet(device(p // 2, z, p % 2, xh, y))
    for par in range(2):
        src_z = 2 * y + par

        @pl.when(src_z != z)
        def _():
            for t in range(NT):
                greet(device(xl, src_z, c, t // 4, t % 4))

    wl[pl.ds(64, 64), :] = jnp.zeros((64, wl.shape[1]), wl.dtype)
    wr[pl.ds(0, 64), :] = jnp.zeros((64, wr.shape[1]), wr.dtype)
    tiles[...] = jnp.zeros_like(tiles)
    win.wait()
    wout.wait()

    def project(off):
        for copy in load(off):
            copy.wait()
        part[off] = contract_last(hbuf[off], wl[...]) + contract_last(obuf[off], wr[...])

    def rs_copy(off):
        t = peer(off)
        return pltpu.make_async_remote_copy(
            src_ref=part.at[off], dst_ref=recv.at[off], send_sem=rs_send.at[off], recv_sem=rs_recv.at[off],
            device_id=device(xl, z, c, t // 4, t % 4), device_id_type=MESH,
        )

    project(NT - 1)
    pl.semaphore_wait(barrier, (NT - 1) + (NQ - 1) + 2 * (NZ - 1))
    rs_copy(NT - 1).start()

    def step(j, carry):
        off = NT - 1 - j
        project(off)
        rs_copy(off).start()
        return carry

    lax.fori_loop(1, NT - 1, step, 0)
    project(0)

    total = part[0]
    for off in range(NT - 1, 0, -1):
        rs_copy(off).wait_recv()
    for off in range(1, NT):
        total = total + recv[off]

    scale = 1.0 / math.sqrt(256 * 64)
    gram = lax.dot_general(
        total.T[:64], total, (((1,), (0,)), ((), ())), precision=HIGHEST, preferred_element_type=jnp.float32
    ) * scale
    lane = lax.broadcasted_iota(jnp.int32, (32, 128), 1)
    packed = jnp.where(lane < 64, pltpu.roll(gram[:32], 64, 1), gram[32:])
    fbuf[...] = packed.reshape(NQ, 8, 128)

    def e_copy(j):
        p = q ^ j
        return pltpu.make_async_remote_copy(
            src_ref=fbuf.at[p], dst_ref=ebuf.at[q], send_sem=e_send.at[j], recv_sem=e_recv.at[j],
            device_id=device(p // 2, z, p % 2, xh, y), device_id_type=MESH,
        )

    for j in (2, 3, 1):
        e_copy(j).start()
    ebuf[q] = fbuf[q]
    for j in range(1, NQ):
        e_copy(j).wait_recv()

    def col_copy(dz, a):
        return pltpu.make_async_remote_copy(
            src_ref=ebuf.at[pl.ds(2 * a, 2)], dst_ref=cols.at[zpar, me],
            send_sem=col_send, recv_sem=col_recv.at[zpar],
            device_id=device(xl, lax.rem(z + dz, NZ), c, a, zrow), device_id_type=MESH,
        )

    def row_copy(off):
        t = peer(off)
        return pltpu.make_async_remote_copy(
            src_ref=ebuf, dst_ref=rows.at[:, me], send_sem=row_send, recv_sem=row_recv,
            device_id=device(xl, z, c, t // 4, t % 4), device_id_type=MESH,
        )

    for dz in (4, 3, 5, 2, 6, 1, 7):
        for a in range(2):
            col_copy(dz, a).start()
    for off in range(NT - 1, 0, -1):
        row_copy(off).start()
    rows[:, me] = ebuf[...]

    pltpu.make_async_copy(rows.at[:, pl.ds(0, 7)], rows.at[:, pl.ds(0, 7)], row_recv).wait()
    for par in range(2):

        @pl.when(2 * y + par != z)
        def _():
            pltpu.make_async_copy(cols.at[par], cols.at[par], col_recv.at[par]).wait()

        @pl.when(2 * y + par == z)
        def _():
            for cc in range(2):
                cols[par, :, cc] = rows[2 * xh + cc]

    row_all = rows[...].reshape(32, 8, 128)
    acc = jnp.zeros((32, 32), jnp.float32)
    for r in range(8):
        left = row_all[:, r, :]
        right = jnp.concatenate([cols[par, :, cc, r, :] for par in range(2) for cc in range(2)], axis=0)
        acc = acc + contract_last(left, right, HIGHEST)
    tiles[:, :, pl.ds(0, 32)] = acc.reshape(NQ, 8, 32)

    def t_copy(j):
        p = q ^ j
        return pltpu.make_async_remote_copy(
            src_ref=tiles.at[p], dst_ref=tiles_in.at[q], send_sem=t_send.at[j], recv_sem=t_recv.at[j],
            device_id=device(p // 2, z, p % 2, xh, y), device_id_type=MESH,
        )

    for j in (2, 3, 1):
        t_copy(j).start()
    tiles_in[q] = tiles[q]
    for j in range(1, NQ):
        t_copy(j).wait_recv()
    out_ref[...] = (tiles_in[0] + tiles_in[1] + tiles_in[2] + tiles_in[3])[:, :32]

    for off in range(1, NT):
        rs_copy(off).wait_send()
    for j in range(1, NQ):
        e_copy(j).wait_send()
        t_copy(j).wait_send()
    pltpu.make_async_copy(rows.at[:, pl.ds(0, 7)], rows.at[:, pl.ds(0, 7)], row_send).wait()
    pltpu.make_async_copy(rows.at[:, pl.ds(0, 7)], rows.at[:, pl.ds(0, 7)], col_send).wait()


def per_device(hidden_acts, out_grads, input_basis, output_basis):
    seqs, length, width_ff = hidden_acts.shape
    width_d = out_grads.shape[2]
    f32, bf16 = jnp.float32, jnp.bfloat16
    dma, vmem = pltpu.SemaphoreType.DMA, pltpu.VMEM
    return pl.pallas_call(
        kernel,
        out_shape=jax.ShapeDtypeStruct((8, 32), f32),
        in_specs=[pl.BlockSpec(memory_space=pl.ANY)] * 4,
        out_specs=pl.BlockSpec(memory_space=pltpu.VMEM),
        scratch_shapes=[
            vmem((seqs, length, width_ff), bf16),
            vmem((seqs, length, width_d), bf16),
            vmem((128, width_ff), bf16),
            vmem((128, width_d), bf16),
            vmem((NT, length, 128), f32),
            vmem((NT, length, 128), f32),
            vmem((NQ, 8, 128), f32),
            vmem((NQ, 8, 128), f32),
            vmem((NQ, NT, 8, 128), f32),
            vmem((2, NT, 2, 8, 128), f32),
            vmem((NQ, 8, 128), f32),
            vmem((NQ, 8, 128), f32),
            dma((NT,)), dma((NT,)), dma((2,)),
            dma((NT,)), dma((NT,)),
            dma((NQ,)), dma((NQ,)),
            dma, dma,
            dma, dma((2,)),
            dma((NQ,)), dma((NQ,)),
        ],
        compiler_params=pltpu.CompilerParams(
            collective_id=0, has_side_effects=True, vmem_limit_bytes=48 * 2**20
        ),
        cost_estimate=pl.CostEstimate(flops=700_000_000, bytes_accessed=10_000_000, transcendentals=0),
    )(hidden_acts, out_grads, input_basis, output_basis)


def solution(mesh):
    return jax.shard_map(
        per_device,
        mesh=mesh,
        in_specs=(
            P("dp", None, "tensor"),
            P("dp", None, "tensor"),
            P(None, "tensor"),
            P(None, "tensor"),
        ),
        out_specs=P("dp", "tensor"),
        check_vma=False,
    )
```

```python
import math

import jax
import jax.numpy as jnp
from jax import lax
from jax.experimental import pallas as pl
from jax.experimental.pallas import tpu as pltpu
from jax.sharding import PartitionSpec as P

MESH = pl.DeviceIdType.MESH
HIGHEST = lax.Precision.HIGHEST
NT = 8
NQ = 4
NZ = 8
FROM_X, FROM_YM_O, FROM_YP_O, FROM_YM, FROM_YP, FROM_Y2, FROM_X_SUM = range(7)


def device(xl, z, c, xh, y):
    return {"dp": xl * 16 + z * 2 + c, "tensor": xh * 4 + y}


def contract_last(a, b, precision=None):
    return lax.dot_general(
        a, b, (((1,), (1,)), ((), ())), precision=precision, preferred_element_type=jnp.float32
    )


def kernel(
    h_hbm, o_hbm, pin_hbm, pout_hbm, out_ref,
    hbuf, obuf, wl, wr, part, recv, fbuf, ebuf, rows, cols, tiles, tiles_in,
    hsem, osem, wsem, rs_send, rs_recv, e_send, e_recv, row_send, row_recv, col_send, col_recv, t_send, t_recv,
):
    dp, me = lax.axis_index("dp"), lax.axis_index("tensor")
    xl, z, c = dp // 16, (dp // 2) % 8, dp % 2
    xh, y = me // 4, me % 4
    q = xl * 2 + c
    zpar, zrow = z % 2, z // 2

    def peer(off):
        return lax.rem(xh + off // 4, 2), lax.rem(y + off % 4, 4)

    barrier = pltpu.get_barrier_semaphore()

    def greet(dev):
        pl.semaphore_signal(barrier, inc=1, device_id=dev, device_id_type=MESH)

    for off in range(NT - 1, 0, -1):
        greet(device(xl, z, c, *peer(off)))
    for off in range(NT - 1, -1, -1):
        greet(device(1 - xl, z, c, *peer(off)))
    greet(device(xl, z, 1 - c, xh, y))
    greet(device(1 - xl, z, 1 - c, xh, y))
    for par in range(2):
        src_z = 2 * y + par

        @pl.when(src_z != z)
        def _():
            for t in range(NT):
                greet(device(xh, src_z, c, t // 4, t % 4))

    greetings = 7 + 8 + 2 + 2 * (NZ - 1)

    win = pltpu.make_async_copy(pin_hbm, wl, wsem.at[0])
    wout = pltpu.make_async_copy(pout_hbm, wr, wsem.at[1])

    def load(off):
        a, b = peer(off)
        return (
            pltpu.make_async_copy(h_hbm.at[a * 4 + b], hbuf.at[off], hsem.at[off]),
            pltpu.make_async_copy(o_hbm.at[a * 4 + b], obuf.at[off], osem.at[off]),
        )

    win.start()
    wout.start()
    for off in (6, 5, 7, 4, 1, 3, 2, 0):
        for copy in load(off):
            copy.start()
    tiles[...] = jnp.zeros_like(tiles)
    win.wait()
    wout.wait()

    def project(off):
        for copy in load(off):
            copy.wait()
        part[off, pl.ds(0, 64)] = contract_last(wl[...], hbuf[off])
        part[off, pl.ds(64, 64)] = contract_last(wr[...], obuf[off])

    def rs_copy(off, half, slot, to):
        rowset = pl.ds(64 * half, 64)
        a, b = peer(to)
        return pltpu.make_async_remote_copy(
            src_ref=part.at[off, rowset], dst_ref=recv.at[slot, rowset],
            send_sem=rs_send.at[slot, half], recv_sem=rs_recv.at[slot, half],
            device_id=device(xl, z, c, a, b), device_id_type=MESH,
        )

    x_first = (6, FROM_X, 4)
    o_up, o_down = (5, FROM_YM_O, 1), (7, FROM_YP_O, 3)
    s_up, s_down = (1, FROM_YM, 1), (3, FROM_YP, 3)
    s_across = (2, FROM_Y2, 2)
    x_sum = (4, FROM_X_SUM, 4)

    def start(msg, half):
        rs_copy(msg[0], half, msg[1], msg[2]).start()

    def arrived(msg, half):
        rs_copy(msg[0], half, msg[1], msg[2]).wait_recv()

    for off in (6, 5, 7, 4):
        project(off)
    pl.semaphore_wait(barrier, greetings)
    for half in range(2):
        start(x_first, half)
        start(o_up, half)
        start(o_down, half)
    project(1)
    project(3)
    for half in range(2):
        start(s_up, half)
        start(s_down, half)
    project(2)
    for half in range(2):
        rowset = pl.ds(64 * half, 64)
        arrived(o_up, half)
        arrived(o_down, half)
        part[4, rowset] += recv[FROM_YM_O, rowset] + recv[FROM_YP_O, rowset]
        start(x_sum, half)
        arrived(x_first, half)
        part[2, rowset] += recv[FROM_X, rowset]
        start(s_across, half)
    project(0)
    for msg in (s_up, s_down, x_sum, s_across):
        for half in range(2):
            arrived(msg, half)
    total = (part[0] + recv[FROM_YM]) + (recv[FROM_YP] + recv[FROM_X_SUM]) + recv[FROM_Y2]

    scale = 1.0 / math.sqrt(256 * 64)
    right = total[64:]
    gram = contract_last(total[:64], jnp.concatenate([right, right], axis=0), HIGHEST) * scale
    lane = lax.broadcasted_iota(jnp.int32, (32, 128), 1)
    fbuf[...] = jnp.where(lane < 64, gram[:32], gram[32:]).reshape(2, 2, 8, 128)

    e_copy = pltpu.make_async_remote_copy(
        src_ref=fbuf.at[1 - c], dst_ref=ebuf.at[c], send_sem=e_send, recv_sem=e_recv,
        device_id=device(xl, z, 1 - c, xh, y), device_id_type=MESH,
    )
    e_copy.start()
    ebuf[c] = fbuf[c]
    e_copy.wait_recv()

    def col_copy(dz, to_xl):
        return pltpu.make_async_remote_copy(
            src_ref=ebuf.at[:, to_xl], dst_ref=cols.at[zpar, me],
            send_sem=col_send, recv_sem=col_recv.at[zpar],
            device_id=device(to_xl, lax.rem(z + dz, NZ), c, xl, zrow), device_id_type=MESH,
        )

    def row_copy(off, to_xl):
        return pltpu.make_async_remote_copy(
            src_ref=ebuf.at[:, to_xl], dst_ref=rows.at[pl.ds(2 * xl, 2), me],
            send_sem=row_send, recv_sem=row_recv,
            device_id=device(to_xl, z, c, *peer(off)), device_id_type=MESH,
        )

    for dz in (4, 3, 5, 2, 6, 1, 7):
        for to_xl in (xl, 1 - xl):
            col_copy(dz, to_xl).start()
    for off in range(NT - 1, 0, -1):
        row_copy(off, xl).start()
    for off in range(NT - 1, -1, -1):
        row_copy(off, 1 - xl).start()
    rows[pl.ds(2 * xl, 2), me] = ebuf[:, xl]

    row_bytes = rows.reshape(32, 8, 128).at[pl.ds(0, 30)]
    pltpu.make_async_copy(row_bytes, row_bytes, row_recv).wait()
    for par in range(2):

        @pl.when(2 * y + par != z)
        def _():
            pltpu.make_async_copy(cols.at[par], cols.at[par], col_recv.at[par]).wait()

        @pl.when(2 * y + par == z)
        def _():
            for cc in range(2):
                cols[par, :, cc] = rows[2 * xh + cc]

    row_all = rows[...].reshape(32, 8, 128)
    acc = jnp.zeros((32, 32), jnp.float32)
    for r in range(8):
        col_r = jnp.concatenate([cols[par, :, cc, r, :] for par in range(2) for cc in range(2)], axis=0)
        acc = acc + contract_last(row_all[:, r, :], col_r, HIGHEST)
    tiles[:, :, pl.ds(0, 32)] = acc.reshape(NQ, 8, 32)

    def t_copy(j):
        p = q ^ j
        return pltpu.make_async_remote_copy(
            src_ref=tiles.at[p], dst_ref=tiles_in.at[q], send_sem=t_send.at[j], recv_sem=t_recv.at[j],
            device_id=device(p // 2, z, p % 2, xh, y), device_id_type=MESH,
        )

    for j in (3, 2, 1):
        t_copy(j).start()
    tiles_in[q] = tiles[q]
    for j in range(1, NQ):
        t_copy(j).wait_recv()
    out_ref[...] = (tiles_in[0] + tiles_in[1] + tiles_in[2] + tiles_in[3])[:, :32]

    for msg in (x_first, o_up, o_down, s_up, s_down, s_across, x_sum):
        for half in range(2):
            rs_copy(msg[0], half, msg[1], msg[2]).wait_send()
    e_copy.wait_send()
    for j in range(1, NQ):
        t_copy(j).wait_send()
    pltpu.make_async_copy(row_bytes, row_bytes, row_send).wait()
    col_bytes = rows.reshape(32, 8, 128).at[pl.ds(0, 28)]
    pltpu.make_async_copy(col_bytes, col_bytes, col_send).wait()


def per_device(hidden_acts, out_grads, input_basis, output_basis):
    seqs, length, width_ff = hidden_acts.shape
    width_d = out_grads.shape[2]
    f32, bf16 = jnp.float32, jnp.bfloat16
    dma, vmem = pltpu.SemaphoreType.DMA, pltpu.VMEM
    return pl.pallas_call(
        kernel,
        out_shape=jax.ShapeDtypeStruct((8, 32), f32),
        in_specs=[pl.BlockSpec(memory_space=pltpu.HBM)] * 4,
        out_specs=pl.BlockSpec(memory_space=pltpu.VMEM),
        scratch_shapes=[
            vmem((seqs, length, width_ff), bf16),
            vmem((seqs, length, width_d), bf16),
            vmem((64, width_ff), bf16),
            vmem((64, width_d), bf16),
            vmem((NT, 128, length), f32),
            vmem((7, 128, length), f32),
            vmem((2, 2, 8, 128), f32),
            vmem((2, 2, 8, 128), f32),
            vmem((NQ, NT, 8, 128), f32),
            vmem((2, NT, 2, 8, 128), f32),
            vmem((NQ, 8, 128), f32),
            vmem((NQ, 8, 128), f32),
            dma((NT,)), dma((NT,)), dma((2,)),
            dma((7, 2)), dma((7, 2)),
            dma, dma,
            dma, dma,
            dma, dma((2,)),
            dma((NQ,)), dma((NQ,)),
        ],
        compiler_params=pltpu.CompilerParams(
            collective_id=0, has_side_effects=True, vmem_limit_bytes=62 * 2**20
        ),
        cost_estimate=pl.CostEstimate(flops=700_000_000, bytes_accessed=10_000_000, transcendentals=0),
    )(hidden_acts, out_grads, input_basis, output_basis)


def solution(mesh):
    return jax.shard_map(
        per_device,
        mesh=mesh,
        in_specs=(
            P("dp", None, "tensor"),
            P("dp", None, "tensor"),
            P(None, "tensor"),
            P(None, "tensor"),
        ),
        out_specs=P("dp", "tensor"),
        check_vma=False,
    )
```

```python
import math

import jax
import jax.numpy as jnp
from jax import lax
from jax.experimental import pallas as pl
from jax.experimental.pallas import tpu as pltpu
from jax.sharding import PartitionSpec as P

MESH = pl.DeviceIdType.MESH
HIGHEST = lax.Precision.HIGHEST
NT = 8
NQ = 4
NZ = 8
ORDER = (6, 5, 7, 4, 1, 3, 2, 0)
DEPTH = 3
FROM_X, FROM_YM_O, FROM_YP_O, FROM_YM, FROM_YP, FROM_Y2, FROM_X_SUM = range(7)


def device(xl, z, c, xh, y):
    return {"dp": xl * 16 + z * 2 + c, "tensor": xh * 4 + y}


def contract_last(a, b, precision=None):
    return lax.dot_general(
        a, b, (((1,), (1,)), ((), ())), precision=precision, preferred_element_type=jnp.float32
    )


def kernel(
    h_hbm, o_hbm, pin_hbm, pout_hbm, out_ref,
    hbuf, obuf, wl, wr, part, recv, fbuf, ebuf, rows, cols, tiles, tiles_in,
    hsem, osem, wsem, rs_send, rs_recv, e_send, e_recv, row_send, row_recv, col_send, col_recv, t_send, t_recv, line_sem,
):
    dp, me = lax.axis_index("dp"), lax.axis_index("tensor")
    xl, z, c = dp // 16, (dp // 2) % 8, dp % 2
    xh, y = me // 4, me % 4
    q = xl * 2 + c
    zpar, zrow = z % 2, z // 2

    def peer(off):
        return lax.rem(xh + off // 4, 2), lax.rem(y + off % 4, 4)

    win = pltpu.make_async_copy(pin_hbm, wl, wsem.at[0])
    wout = pltpu.make_async_copy(pout_hbm, wr, wsem.at[1])

    def load(off):
        a, b = peer(off)
        return (
            pltpu.make_async_copy(h_hbm.at[a * 4 + b], hbuf.at[off], hsem.at[off]),
            pltpu.make_async_copy(o_hbm.at[a * 4 + b], obuf.at[off], osem.at[off]),
        )

    win.start()
    wout.start()
    for off in ORDER[:DEPTH]:
        for copy in load(off):
            copy.start()

    barrier = pltpu.get_barrier_semaphore()

    def greet(dev):
        pl.semaphore_signal(barrier, inc=1, device_id=dev, device_id_type=MESH)

    for off in range(NT - 1, 0, -1):
        greet(device(xl, z, c, *peer(off)))
    for off in range(NT - 1, -1, -1):
        greet(device(1 - xl, z, c, *peer(off)))
    greet(device(xl, z, 1 - c, xh, y))
    greet(device(1 - xl, z, 1 - c, xh, y))
    for dz in (4, 3, 5, 2, 6, 1, 7):
        greet(device(xl, lax.rem(z + dz, NZ), c, xh, y))
    greetings = 7 + 8 + 2 + 7

    tiles[...] = jnp.zeros_like(tiles)
    win.wait()
    wout.wait()

    def project(off):
        for copy in load(off):
            copy.wait()
        ahead = ORDER.index(off) + DEPTH
        if ahead < NT:
            for copy in load(ORDER[ahead]):
                copy.start()
        part[off, pl.ds(0, 64)] = contract_last(wl[...], hbuf[off])
        part[off, pl.ds(64, 64)] = contract_last(wr[...], obuf[off])

    def rs_copy(off, half, slot, to):
        rowset = pl.ds(64 * half, 64)
        a, b = peer(to)
        return pltpu.make_async_remote_copy(
            src_ref=part.at[off, rowset], dst_ref=recv.at[slot, rowset],
            send_sem=rs_send.at[slot, half], recv_sem=rs_recv.at[slot, half],
            device_id=device(xl, z, c, a, b), device_id_type=MESH,
        )

    x_first = (6, FROM_X, 4)
    o_up, o_down = (5, FROM_YM_O, 1), (7, FROM_YP_O, 3)
    s_up, s_down = (1, FROM_YM, 1), (3, FROM_YP, 3)
    s_across = (2, FROM_Y2, 2)
    x_sum = (4, FROM_X_SUM, 4)

    def start(msg, half):
        rs_copy(msg[0], half, msg[1], msg[2]).start()

    def arrived(msg, half):
        rs_copy(msg[0], half, msg[1], msg[2]).wait_recv()

    for off in (6, 5, 7, 4):
        project(off)
    pl.semaphore_wait(barrier, greetings)

    @pl.when(y == zrow)
    def _():
        for t in range(NT):

            @pl.when((xl != xh) | (me != t))
            def _():
                pl.semaphore_signal(
                    line_sem, inc=1, device_id=device(xh, z, c, t // 4, t % 4), device_id_type=MESH
                )

    for half in range(2):
        start(x_first, half)
        start(o_up, half)
        start(o_down, half)
    project(1)
    project(3)
    for half in range(2):
        start(s_up, half)
        start(s_down, half)
    project(2)
    for half in range(2):
        rowset = pl.ds(64 * half, 64)
        arrived(o_up, half)
        arrived(o_down, half)
        part[4, rowset] += recv[FROM_YM_O, rowset] + recv[FROM_YP_O, rowset]
        start(x_sum, half)
        arrived(x_first, half)
        part[2, rowset] += recv[FROM_X, rowset]
        start(s_across, half)
    project(0)
    for msg in (s_up, s_down, x_sum, s_across):
        for half in range(2):
            arrived(msg, half)
    total = (part[0] + recv[FROM_YM]) + (recv[FROM_YP] + recv[FROM_X_SUM]) + recv[FROM_Y2]

    scale = 1.0 / math.sqrt(256 * 64)
    right = total[64:]
    gram = contract_last(total[:64], jnp.concatenate([right, right], axis=0), HIGHEST) * scale
    lane = lax.broadcasted_iota(jnp.int32, (32, 128), 1)
    fbuf[...] = jnp.where(lane < 64, gram[:32], gram[32:]).reshape(2, 2, 8, 128)

    e_copy = pltpu.make_async_remote_copy(
        src_ref=fbuf.at[1 - c], dst_ref=ebuf.at[c], send_sem=e_send, recv_sem=e_recv,
        device_id=device(xl, z, 1 - c, xh, y), device_id_type=MESH,
    )
    e_copy.start()
    ebuf[c] = fbuf[c]
    e_copy.wait_recv()

    def col_copy(dz, to_xl):
        return pltpu.make_async_remote_copy(
            src_ref=ebuf.at[:, to_xl], dst_ref=cols.at[zpar, me],
            send_sem=col_send, recv_sem=col_recv.at[zpar],
            device_id=device(to_xl, lax.rem(z + dz, NZ), c, xl, zrow), device_id_type=MESH,
        )

    def row_copy(off, to_xl):
        return pltpu.make_async_remote_copy(
            src_ref=ebuf.at[:, to_xl], dst_ref=rows.at[pl.ds(2 * xl, 2), me],
            send_sem=row_send, recv_sem=row_recv,
            device_id=device(to_xl, z, c, *peer(off)), device_id_type=MESH,
        )

    own_line = ((xh == xl) & (y == zrow)).astype(jnp.int32)
    pl.semaphore_wait(line_sem, 2 - own_line)
    for dz in (4, 3, 5, 2, 6, 1, 7):
        for to_xl in (xl, 1 - xl):
            col_copy(dz, to_xl).start()
    for off in range(NT - 1, 0, -1):
        row_copy(off, xl).start()
    for off in range(NT - 1, -1, -1):
        row_copy(off, 1 - xl).start()
    rows[pl.ds(2 * xl, 2), me] = ebuf[:, xl]

    row_bytes = rows.reshape(32, 8, 128).at[pl.ds(0, 30)]
    pltpu.make_async_copy(row_bytes, row_bytes, row_recv).wait()
    for par in range(2):

        @pl.when(2 * y + par != z)
        def _():
            pltpu.make_async_copy(cols.at[par], cols.at[par], col_recv.at[par]).wait()

        @pl.when(2 * y + par == z)
        def _():
            for cc in range(2):
                cols[par, :, cc] = rows[2 * xh + cc]

    row_all = rows[...].reshape(32, 8, 128)
    acc = jnp.zeros((32, 32), jnp.float32)
    for r in range(8):
        col_r = jnp.concatenate([cols[par, :, cc, r, :] for par in range(2) for cc in range(2)], axis=0)
        acc = acc + contract_last(row_all[:, r, :], col_r, HIGHEST)
    tiles[:, :, pl.ds(0, 32)] = acc.reshape(NQ, 8, 32)

    def t_copy(j):
        p = q ^ j
        return pltpu.make_async_remote_copy(
            src_ref=tiles.at[p], dst_ref=tiles_in.at[q], send_sem=t_send.at[j], recv_sem=t_recv.at[j],
            device_id=device(p // 2, z, p % 2, xh, y), device_id_type=MESH,
        )

    for j in (3, 2, 1):
        t_copy(j).start()
    tiles_in[q] = tiles[q]
    for j in range(1, NQ):
        t_copy(j).wait_recv()
    out_ref[...] = (tiles_in[0] + tiles_in[1] + tiles_in[2] + tiles_in[3])[:, :32]

    for msg in (x_first, o_up, o_down, s_up, s_down, s_across, x_sum):
        for half in range(2):
            rs_copy(msg[0], half, msg[1], msg[2]).wait_send()
    e_copy.wait_send()
    for j in range(1, NQ):
        t_copy(j).wait_send()
    pltpu.make_async_copy(row_bytes, row_bytes, row_send).wait()
    col_bytes = rows.reshape(32, 8, 128).at[pl.ds(0, 28)]
    pltpu.make_async_copy(col_bytes, col_bytes, col_send).wait()


def per_device(hidden_acts, out_grads, input_basis, output_basis):
    seqs, length, width_ff = hidden_acts.shape
    width_d = out_grads.shape[2]
    f32, bf16 = jnp.float32, jnp.bfloat16
    dma, vmem = pltpu.SemaphoreType.DMA, pltpu.VMEM
    return pl.pallas_call(
        kernel,
        out_shape=jax.ShapeDtypeStruct((8, 32), f32),
        in_specs=[pl.BlockSpec(memory_space=pltpu.HBM)] * 4,
        out_specs=pl.BlockSpec(memory_space=pltpu.VMEM),
        scratch_shapes=[
            vmem((seqs, length, width_ff), bf16),
            vmem((seqs, length, width_d), bf16),
            vmem((64, width_ff), bf16),
            vmem((64, width_d), bf16),
            vmem((NT, 128, length), f32),
            vmem((7, 128, length), f32),
            vmem((2, 2, 8, 128), f32),
            vmem((2, 2, 8, 128), f32),
            vmem((NQ, NT, 8, 128), f32),
            vmem((2, NT, 2, 8, 128), f32),
            vmem((NQ, 8, 128), f32),
            vmem((NQ, 8, 128), f32),
            dma((NT,)), dma((NT,)), dma((2,)),
            dma((7, 2)), dma((7, 2)),
            dma, dma,
            dma, dma,
            dma, dma((2,)),
            dma((NQ,)), dma((NQ,)),
            pltpu.SemaphoreType.REGULAR,
        ],
        compiler_params=pltpu.CompilerParams(
            collective_id=0, has_side_effects=True, vmem_limit_bytes=62 * 2**20
        ),
        cost_estimate=pl.CostEstimate(flops=700_000_000, bytes_accessed=10_000_000, transcendentals=0),
    )(hidden_acts, out_grads, input_basis, output_basis)


def solution(mesh):
    return jax.shard_map(
        per_device,
        mesh=mesh,
        in_specs=(
            P("dp", None, "tensor"),
            P("dp", None, "tensor"),
            P(None, "tensor"),
            P(None, "tensor"),
        ),
        out_specs=P("dp", "tensor"),
        check_vma=False,
    )
```

```python
import math

import jax
import jax.numpy as jnp
from jax import lax
from jax.experimental import pallas as pl
from jax.experimental.pallas import tpu as pltpu
from jax.sharding import PartitionSpec as P

MESH = pl.DeviceIdType.MESH
HIGHEST = lax.Precision.HIGHEST
NT = 8
NQ = 4
NZ = 8
ORDER = (6, 5, 7, 1, 3, 4, 2, 0)
DEPTH = 3
FROM_X, FROM_YM_O, FROM_YP_O, FROM_YM, FROM_YP, FROM_Y2, FROM_X_SUM = range(7)


def device(xl, z, c, xh, y):
    return {"dp": xl * 16 + z * 2 + c, "tensor": xh * 4 + y}


def contract_last(a, b, precision=None):
    return lax.dot_general(
        a, b, (((1,), (1,)), ((), ())), precision=precision, preferred_element_type=jnp.float32
    )


def kernel(
    h_hbm, o_hbm, pin_hbm, pout_hbm, out_ref,
    hbuf, obuf, wl, wr, part, recv, fbuf, ebuf, rows, cols, tiles, tiles_in,
    hsem, osem, wsem, rs_send, rs_recv, e_send, e_recv, row_send, row_recv, col_send, col_recv, t_send, t_recv, line_sem, z_sem, xl_sem,
):
    dp, me = lax.axis_index("dp"), lax.axis_index("tensor")
    xl, z, c = dp // 16, (dp // 2) % 8, dp % 2
    xh, y = me // 4, me % 4
    q = xl * 2 + c
    zpar, zrow = z % 2, z // 2

    def peer(off):
        return lax.rem(xh + off // 4, 2), lax.rem(y + off % 4, 4)

    win = pltpu.make_async_copy(pin_hbm, wl, wsem.at[0])
    wout = pltpu.make_async_copy(pout_hbm, wr, wsem.at[1])

    def load(off):
        a, b = peer(off)
        return (
            pltpu.make_async_copy(h_hbm.at[a * 4 + b], hbuf.at[off], hsem.at[off]),
            pltpu.make_async_copy(o_hbm.at[a * 4 + b], obuf.at[off], osem.at[off]),
        )

    win.start()
    wout.start()
    for off in ORDER[:DEPTH]:
        for copy in load(off):
            copy.start()

    barrier = pltpu.get_barrier_semaphore()

    def greet(dev):
        pl.semaphore_signal(barrier, inc=1, device_id=dev, device_id_type=MESH)

    near = [device(xl, z, c, *peer(off)) for off in (4, 2, 1, 3)]
    near_z = [device(xl, lax.rem(z + dz, NZ), c, xh, y) for dz in (2, 6, 1, 7)]
    other_xl = device(1 - xl, z, c, xh, y)
    for dev in near + [device(1 - xl, z, 1 - c, xh, y)] + near_z + [other_xl, device(xl, z, 1 - c, xh, y)]:
        greet(dev)
    greetings = 11

    tiles[...] = jnp.zeros_like(tiles)
    win.wait()
    wout.wait()

    def project(off):
        for copy in load(off):
            copy.wait()
        ahead = ORDER.index(off) + DEPTH
        if ahead < NT:
            for copy in load(ORDER[ahead]):
                copy.start()
        part[off, pl.ds(0, 64)] = contract_last(wl[...], hbuf[off])
        part[off, pl.ds(64, 64)] = contract_last(wr[...], obuf[off])

    def rs_copy(off, half, slot, to):
        rowset = pl.ds(64 * half, 64)
        a, b = peer(to)
        return pltpu.make_async_remote_copy(
            src_ref=part.at[off, rowset], dst_ref=recv.at[slot, rowset],
            send_sem=rs_send.at[slot, half], recv_sem=rs_recv.at[slot, half],
            device_id=device(xl, z, c, a, b), device_id_type=MESH,
        )

    x_first = (6, FROM_X, 4)
    o_up, o_down = (5, FROM_YM_O, 1), (7, FROM_YP_O, 3)
    s_up, s_down = (1, FROM_YM, 1), (3, FROM_YP, 3)
    s_across = (2, FROM_Y2, 2)
    x_sum = (4, FROM_X_SUM, 4)

    def start(msg, half):
        rs_copy(msg[0], half, msg[1], msg[2]).start()

    def arrived(msg, half):
        rs_copy(msg[0], half, msg[1], msg[2]).wait_recv()

    for off in (6, 5, 7):
        project(off)
    pl.semaphore_wait(barrier, greetings)
    for half in range(2):
        start(x_first, half)
        start(o_up, half)
        start(o_down, half)
    for dev in near_z:
        pl.semaphore_signal(z_sem, inc=1, device_id=dev, device_id_type=MESH)
    project(1)
    project(3)
    for half in range(2):
        start(s_up, half)
        start(s_down, half)
    project(4)
    project(2)
    for half in range(2):
        rowset = pl.ds(64 * half, 64)
        arrived(o_up, half)
        arrived(o_down, half)
        part[4, rowset] += recv[FROM_YM_O, rowset] + recv[FROM_YP_O, rowset]
        start(x_sum, half)
        arrived(x_first, half)
        part[2, rowset] += recv[FROM_X, rowset]
        start(s_across, half)
        if half == 0:
            pl.semaphore_signal(xl_sem, inc=1, device_id=other_xl, device_id_type=MESH)

    pl.semaphore_wait(z_sem, 4)
    pl.semaphore_wait(xl_sem, 1)

    @pl.when(y == zrow)
    def _():
        for t in range(NT):

            @pl.when((xl != xh) | (me != t))
            def _():
                pl.semaphore_signal(
                    line_sem, inc=1, device_id=device(xh, z, c, t // 4, t % 4), device_id_type=MESH
                )
    project(0)
    for msg in (s_up, s_down, x_sum, s_across):
        for half in range(2):
            arrived(msg, half)
    total = (part[0] + recv[FROM_YM]) + (recv[FROM_YP] + recv[FROM_X_SUM]) + recv[FROM_Y2]

    scale = 1.0 / math.sqrt(256 * 64)
    right = total[64:]
    gram = contract_last(total[:64], jnp.concatenate([right, right], axis=0), HIGHEST) * scale
    lane = lax.broadcasted_iota(jnp.int32, (32, 128), 1)
    fbuf[...] = jnp.where(lane < 64, gram[:32], gram[32:]).reshape(2, 2, 8, 128)

    e_copy = pltpu.make_async_remote_copy(
        src_ref=fbuf.at[1 - c], dst_ref=ebuf.at[c], send_sem=e_send, recv_sem=e_recv,
        device_id=device(xl, z, 1 - c, xh, y), device_id_type=MESH,
    )
    e_copy.start()
    ebuf[c] = fbuf[c]
    e_copy.wait_recv()

    def col_copy(dz, to_xl):
        return pltpu.make_async_remote_copy(
            src_ref=ebuf.at[:, to_xl], dst_ref=cols.at[zpar, me],
            send_sem=col_send, recv_sem=col_recv.at[zpar],
            device_id=device(to_xl, lax.rem(z + dz, NZ), c, xl, zrow), device_id_type=MESH,
        )

    def row_copy(off, to_xl):
        return pltpu.make_async_remote_copy(
            src_ref=ebuf.at[:, to_xl], dst_ref=rows.at[pl.ds(2 * xl, 2), me],
            send_sem=row_send, recv_sem=row_recv,
            device_id=device(to_xl, z, c, *peer(off)), device_id_type=MESH,
        )

    own_line = ((xh == xl) & (y == zrow)).astype(jnp.int32)
    pl.semaphore_wait(line_sem, 2 - own_line)
    for dz in (4, 3, 5, 2, 6, 1, 7):
        for to_xl in (xl, 1 - xl):
            col_copy(dz, to_xl).start()
    for off in range(NT - 1, 0, -1):
        row_copy(off, xl).start()
    for off in range(NT - 1, -1, -1):
        row_copy(off, 1 - xl).start()
    rows[pl.ds(2 * xl, 2), me] = ebuf[:, xl]

    row_bytes = rows.reshape(32, 8, 128).at[pl.ds(0, 30)]
    pltpu.make_async_copy(row_bytes, row_bytes, row_recv).wait()
    for par in range(2):

        @pl.when(2 * y + par != z)
        def _():
            pltpu.make_async_copy(cols.at[par], cols.at[par], col_recv.at[par]).wait()

        @pl.when(2 * y + par == z)
        def _():
            for cc in range(2):
                cols[par, :, cc] = rows[2 * xh + cc]

    row_all = rows[...].reshape(32, 8, 128)
    acc = jnp.zeros((32, 32), jnp.float32)
    for r in range(8):
        col_r = jnp.concatenate([cols[par, :, cc, r, :] for par in range(2) for cc in range(2)], axis=0)
        acc = acc + contract_last(row_all[:, r, :], col_r, HIGHEST)
    tiles[:, :, pl.ds(0, 32)] = acc.reshape(NQ, 8, 32)

    def t_copy(j):
        p = q ^ j
        return pltpu.make_async_remote_copy(
            src_ref=tiles.at[p], dst_ref=tiles_in.at[q], send_sem=t_send.at[j], recv_sem=t_recv.at[j],
            device_id=device(p // 2, z, p % 2, xh, y), device_id_type=MESH,
        )

    for j in (3, 2, 1):
        t_copy(j).start()
    tiles_in[q] = tiles[q]
    for j in range(1, NQ):
        t_copy(j).wait_recv()
    out_ref[...] = (tiles_in[0] + tiles_in[1] + tiles_in[2] + tiles_in[3])[:, :32]

    for msg in (x_first, o_up, o_down, s_up, s_down, s_across, x_sum):
        for half in range(2):
            rs_copy(msg[0], half, msg[1], msg[2]).wait_send()
    e_copy.wait_send()
    for j in range(1, NQ):
        t_copy(j).wait_send()
    pltpu.make_async_copy(row_bytes, row_bytes, row_send).wait()
    col_bytes = rows.reshape(32, 8, 128).at[pl.ds(0, 28)]
    pltpu.make_async_copy(col_bytes, col_bytes, col_send).wait()


def per_device(hidden_acts, out_grads, input_basis, output_basis):
    seqs, length, width_ff = hidden_acts.shape
    width_d = out_grads.shape[2]
    f32, bf16 = jnp.float32, jnp.bfloat16
    dma, vmem = pltpu.SemaphoreType.DMA, pltpu.VMEM
    return pl.pallas_call(
        kernel,
        out_shape=jax.ShapeDtypeStruct((8, 32), f32),
        in_specs=[pl.BlockSpec(memory_space=pltpu.HBM)] * 4,
        out_specs=pl.BlockSpec(memory_space=pltpu.VMEM),
        scratch_shapes=[
            vmem((seqs, length, width_ff), bf16),
            vmem((seqs, length, width_d), bf16),
            vmem((64, width_ff), bf16),
            vmem((64, width_d), bf16),
            vmem((NT, 128, length), f32),
            vmem((7, 128, length), f32),
            vmem((2, 2, 8, 128), f32),
            vmem((2, 2, 8, 128), f32),
            vmem((NQ, NT, 8, 128), f32),
            vmem((2, NT, 2, 8, 128), f32),
            vmem((NQ, 8, 128), f32),
            vmem((NQ, 8, 128), f32),
            dma((NT,)), dma((NT,)), dma((2,)),
            dma((7, 2)), dma((7, 2)),
            dma, dma,
            dma, dma,
            dma, dma((2,)),
            dma((NQ,)), dma((NQ,)),
            pltpu.SemaphoreType.REGULAR, pltpu.SemaphoreType.REGULAR, pltpu.SemaphoreType.REGULAR,
        ],
        compiler_params=pltpu.CompilerParams(
            collective_id=0, has_side_effects=True, vmem_limit_bytes=55168 * 1024
        ),
        cost_estimate=pl.CostEstimate(flops=700_000_000, bytes_accessed=10_000_000, transcendentals=0),
    )(hidden_acts, out_grads, input_basis, output_basis)


def solution(mesh):
    return jax.shard_map(
        per_device,
        mesh=mesh,
        in_specs=(
            P("dp", None, "tensor"),
            P("dp", None, "tensor"),
            P(None, "tensor"),
            P(None, "tensor"),
        ),
        out_specs=P("dp", "tensor"),
        check_vma=False,
    )
```

```python
import math

import jax
import jax.numpy as jnp
from jax import lax
from jax.experimental import pallas as pl
from jax.experimental.pallas import tpu as pltpu
from jax.sharding import PartitionSpec as P

MESH = pl.DeviceIdType.MESH
HIGHEST = lax.Precision.HIGHEST
NT = 8
NQ = 4
NZ = 8
ORDER = (5, 7, 6, 1, 3, 4, 2, 0)
DEPTH = 3
FROM_X, FROM_YM_O, FROM_YP_O, FROM_YM, FROM_YP, FROM_Y2, FROM_X_SUM = range(7)
CUT = 112
X_FIRST = ((6, 0, 64, FROM_X, 4), (6, 64, 64, FROM_X, 4))
X_UP, X_DOWN = (5, CUT, 128 - CUT, FROM_YM_O, 4), (7, CUT, 128 - CUT, FROM_YP_O, 4)
O_UP = tuple((5, r, CUT // 2, FROM_YM_O, 1) for r in (0, CUT // 2))
O_DOWN = tuple((7, r, CUT // 2, FROM_YP_O, 3) for r in (0, CUT // 2))
S_UP = ((1, 0, CUT, FROM_YM, 1), (1, CUT, 128 - CUT, FROM_YM, 1))
S_DOWN = ((3, 0, CUT, FROM_YP, 3), (3, CUT, 128 - CUT, FROM_YP, 3))
S_ACROSS = ((2, 0, 64, FROM_Y2, 2), (2, 64, 64, FROM_Y2, 2))
X_SUM = ((4, 0, CUT // 2, FROM_X_SUM, 4), (4, CUT // 2, CUT // 2, FROM_X_SUM, 4), (4, CUT, 128 - CUT, FROM_X_SUM, 4))
MESSAGES = X_FIRST + (X_UP, X_DOWN) + O_UP + O_DOWN + S_UP + S_DOWN + S_ACROSS + X_SUM


def device(xl, z, c, xh, y):
    return {"dp": xl * 16 + z * 2 + c, "tensor": xh * 4 + y}


def contract_last(a, b, precision=None):
    return lax.dot_general(
        a, b, (((1,), (1,)), ((), ())), precision=precision, preferred_element_type=jnp.float32
    )


def kernel(
    h_hbm, o_hbm, pin_hbm, pout_hbm, out_ref,
    hbuf, obuf, wl, wr, part, recv, fbuf, ebuf, rows, cols, tiles, tiles_in,
    hsem, osem, wsem, rs_send, rs_recv, e_send, e_recv, row_send, row_recv, col_send, col_recv, t_send, t_recv, line_sem, z_sem, xl_sem,
):
    dp, me = lax.axis_index("dp"), lax.axis_index("tensor")
    xl, z, c = dp // 16, (dp // 2) % 8, dp % 2
    xh, y = me // 4, me % 4
    q = xl * 2 + c
    zpar, zrow = z % 2, z // 2

    def peer(off):
        return lax.rem(xh + off // 4, 2), lax.rem(y + off % 4, 4)

    win = pltpu.make_async_copy(pin_hbm, wl, wsem.at[0])
    wout = pltpu.make_async_copy(pout_hbm, wr, wsem.at[1])

    def load(off):
        a, b = peer(off)
        return (
            pltpu.make_async_copy(h_hbm.at[a * 4 + b], hbuf.at[off], hsem.at[off]),
            pltpu.make_async_copy(o_hbm.at[a * 4 + b], obuf.at[off], osem.at[off]),
        )

    win.start()
    wout.start()
    for off in ORDER[:DEPTH]:
        for copy in load(off):
            copy.start()

    barrier = pltpu.get_barrier_semaphore()

    def greet(dev):
        pl.semaphore_signal(barrier, inc=1, device_id=dev, device_id_type=MESH)

    near = [device(xl, z, c, *peer(off)) for off in (4, 2, 1, 3)]
    near_z = [device(xl, lax.rem(z + dz, NZ), c, xh, y) for dz in (2, 6, 1, 7)]
    other_xl = device(1 - xl, z, c, xh, y)
    for dev in near + [device(1 - xl, z, 1 - c, xh, y)] + near_z + [other_xl, device(xl, z, 1 - c, xh, y)]:
        greet(dev)
    greetings = 11

    tiles[...] = jnp.zeros_like(tiles)
    win.wait()
    wout.wait()

    def project(off):
        for copy in load(off):
            copy.wait()
        ahead = ORDER.index(off) + DEPTH
        if ahead < NT:
            for copy in load(ORDER[ahead]):
                copy.start()
        part[off, pl.ds(0, 64)] = contract_last(wl[...], hbuf[off])
        part[off, pl.ds(64, 64)] = contract_last(wr[...], obuf[off])

    def rs_copy(msg):
        chunk, row, count, slot, to = msg
        at = MESSAGES.index(msg)
        return pltpu.make_async_remote_copy(
            src_ref=part.at[chunk, pl.ds(row, count)], dst_ref=recv.at[slot, pl.ds(row, count)],
            send_sem=rs_send.at[at], recv_sem=rs_recv.at[at],
            device_id=device(xl, z, c, *peer(to)), device_id_type=MESH,
        )

    def start(*messages):
        for msg in messages:
            rs_copy(msg).start()

    def arrived(*messages):
        for msg in messages:
            rs_copy(msg).wait_recv()

    for off in (5, 7, 6):
        project(off)
    pl.semaphore_wait(barrier, greetings)
    start(O_UP[0], O_DOWN[0], X_FIRST[0], O_UP[1], O_DOWN[1], X_FIRST[1], X_UP, X_DOWN)
    for dev in near_z:
        pl.semaphore_signal(z_sem, inc=1, device_id=dev, device_id_type=MESH)
    project(1)
    start(S_UP[0])
    project(3)
    start(S_DOWN[0])
    project(4)
    start(X_SUM[2])
    project(2)
    for half in range(2):
        arrived(O_UP[half], O_DOWN[half])
        rowset = pl.ds(CUT // 2 * half, CUT // 2)
        part[4, rowset] += recv[FROM_YM_O, rowset] + recv[FROM_YP_O, rowset]
        start(X_SUM[half])
        arrived(X_FIRST[half])
        rowset = pl.ds(64 * half, 64)
        part[2, rowset] += recv[FROM_X, rowset]
        start(S_ACROSS[half])
        if half == 0:
            pl.semaphore_signal(xl_sem, inc=1, device_id=other_xl, device_id_type=MESH)
    arrived(X_UP, X_DOWN)
    rowset = pl.ds(CUT, 128 - CUT)
    part[1, rowset] += recv[FROM_YM_O, rowset]
    part[3, rowset] += recv[FROM_YP_O, rowset]
    start(S_UP[1], S_DOWN[1])

    pl.semaphore_wait(z_sem, 4)
    pl.semaphore_wait(xl_sem, 1)

    @pl.when(y == zrow)
    def _():
        for t in range(NT):

            @pl.when((xl != xh) | (me != t))
            def _():
                pl.semaphore_signal(
                    line_sem, inc=1, device_id=device(xh, z, c, t // 4, t % 4), device_id_type=MESH
                )
    project(0)
    arrived(*S_UP, *S_DOWN, *X_SUM, *S_ACROSS)
    total = (part[0] + recv[FROM_YM]) + (recv[FROM_YP] + recv[FROM_X_SUM]) + recv[FROM_Y2]

    scale = 1.0 / math.sqrt(256 * 64)
    right = total[64:]
    gram = contract_last(total[:64], jnp.concatenate([right, right], axis=0), HIGHEST) * scale
    lane = lax.broadcasted_iota(jnp.int32, (32, 128), 1)
    fbuf[...] = jnp.where(lane < 64, gram[:32], gram[32:]).reshape(2, 2, 8, 128)

    e_copy = pltpu.make_async_remote_copy(
        src_ref=fbuf.at[1 - c], dst_ref=ebuf.at[:, c], send_sem=e_send, recv_sem=e_recv,
        device_id=device(xl, z, 1 - c, xh, y), device_id_type=MESH,
    )
    e_copy.start()
    ebuf[:, c] = fbuf[c]
    e_copy.wait_recv()

    def col_copy(to_z, to_xl):
        return pltpu.make_async_remote_copy(
            src_ref=ebuf.at[to_xl], dst_ref=cols.at[zpar, me],
            send_sem=col_send, recv_sem=col_recv.at[zpar],
            device_id=device(to_xl, to_z, c, xl, zrow), device_id_type=MESH,
        )

    def row_copy(off, to_xl):
        return pltpu.make_async_remote_copy(
            src_ref=ebuf.at[to_xl], dst_ref=rows.at[xl, me],
            send_sem=row_send, recv_sem=row_recv,
            device_id=device(to_xl, z, c, *peer(off)), device_id_type=MESH,
        )

    own_line = ((xh == xl) & (y == zrow)).astype(jnp.int32)
    pl.semaphore_wait(line_sem, 2 - own_line)
    for i in range(NZ - 1):
        to_z = jnp.where(i < z, i, i + 1)
        for to_xl in (1 - xl, xl):
            col_copy(to_z, to_xl).start()
    for off in range(NT - 1, 0, -1):
        row_copy(off, xl).start()
    for off in range(NT - 1, -1, -1):
        row_copy(off, 1 - xl).start()
    rows[xl, me] = ebuf[xl]

    row_bytes = rows.reshape(32, 8, 128).at[pl.ds(0, 30)]
    pltpu.make_async_copy(row_bytes, row_bytes, row_recv).wait()
    for par in range(2):

        @pl.when(2 * y + par != z)
        def _():
            pltpu.make_async_copy(cols.at[par], cols.at[par], col_recv.at[par]).wait()

        @pl.when(2 * y + par == z)
        def _():
            cols[par] = rows[xh]

    acc = jnp.zeros((32, 32), jnp.float32)
    for r in range(8):
        col_r = jnp.concatenate([cols[par, :, cc, r, :] for par in range(2) for cc in range(2)], axis=0)
        row_r = jnp.concatenate([rows[a, :, cc, r, :] for a in range(2) for cc in range(2)], axis=0)
        acc = acc + contract_last(row_r, col_r, HIGHEST)
    tiles[:, :, pl.ds(0, 32)] = acc.reshape(NQ, 8, 32)

    def t_copy(j):
        p = q ^ j
        return pltpu.make_async_remote_copy(
            src_ref=tiles.at[p], dst_ref=tiles_in.at[q], send_sem=t_send.at[j], recv_sem=t_recv.at[j],
            device_id=device(p // 2, z, p % 2, xh, y), device_id_type=MESH,
        )

    for j in (3, 2, 1):
        t_copy(j).start()
    tiles_in[q] = tiles[q]
    for j in range(1, NQ):
        t_copy(j).wait_recv()
    out_ref[...] = (tiles_in[0] + tiles_in[1] + tiles_in[2] + tiles_in[3])[:, :32]

    for msg in MESSAGES:
        rs_copy(msg).wait_send()
    e_copy.wait_send()
    for j in range(1, NQ):
        t_copy(j).wait_send()
    pltpu.make_async_copy(row_bytes, row_bytes, row_send).wait()
    col_bytes = rows.reshape(32, 8, 128).at[pl.ds(0, 28)]
    pltpu.make_async_copy(col_bytes, col_bytes, col_send).wait()


def per_device(hidden_acts, out_grads, input_basis, output_basis):
    seqs, length, width_ff = hidden_acts.shape
    width_d = out_grads.shape[2]
    f32, bf16 = jnp.float32, jnp.bfloat16
    dma, vmem = pltpu.SemaphoreType.DMA, pltpu.VMEM
    return pl.pallas_call(
        kernel,
        out_shape=jax.ShapeDtypeStruct((8, 32), f32),
        in_specs=[pl.BlockSpec(memory_space=pltpu.HBM)] * 4,
        out_specs=pl.BlockSpec(memory_space=pltpu.VMEM),
        scratch_shapes=[
            vmem((seqs, length, width_ff), bf16),
            vmem((seqs, length, width_d), bf16),
            vmem((64, width_ff), bf16),
            vmem((64, width_d), bf16),
            vmem((NT, 128, length), f32),
            vmem((7, 128, length), f32),
            vmem((2, 2, 8, 128), f32),
            vmem((2, 2, 8, 128), f32),
            vmem((2, NT, 2, 8, 128), f32),
            vmem((2, NT, 2, 8, 128), f32),
            vmem((NQ, 8, 128), f32),
            vmem((NQ, 8, 128), f32),
            dma((NT,)), dma((NT,)), dma((2,)),
            dma((len(MESSAGES),)), dma((len(MESSAGES),)),
            dma, dma,
            dma, dma,
            dma, dma((2,)),
            dma((NQ,)), dma((NQ,)),
            pltpu.SemaphoreType.REGULAR, pltpu.SemaphoreType.REGULAR, pltpu.SemaphoreType.REGULAR,
        ],
        compiler_params=pltpu.CompilerParams(
            collective_id=0, has_side_effects=True, vmem_limit_bytes=55168 * 1024
        ),
        cost_estimate=pl.CostEstimate(flops=700_000_000, bytes_accessed=10_000_000, transcendentals=0),
    )(hidden_acts, out_grads, input_basis, output_basis)


def solution(mesh):
    return jax.shard_map(
        per_device,
        mesh=mesh,
        in_specs=(
            P("dp", None, "tensor"),
            P("dp", None, "tensor"),
            P(None, "tensor"),
            P(None, "tensor"),
        ),
        out_specs=P("dp", "tensor"),
        check_vma=False,
    )
```

```python
import math

import jax
import jax.numpy as jnp
from jax import lax
from jax.experimental import pallas as pl
from jax.experimental.pallas import tpu as pltpu
from jax.sharding import PartitionSpec as P

MESH = pl.DeviceIdType.MESH
HIGHEST = lax.Precision.HIGHEST
NT = 8
NQ = 4
NZ = 8
ORDER = (5, 7, 6, 1, 3, 4, 2, 0)
DEPTH = 3
FROM_X, FROM_YM_O, FROM_YP_O, FROM_YM, FROM_YP, FROM_Y2, FROM_X_SUM = range(7)
CUT = 112
X_FIRST = ((6, 0, 64, FROM_X, 4), (6, 64, 64, FROM_X, 4))
X_UP, X_DOWN = (5, CUT, 128 - CUT, FROM_YM_O, 4), (7, CUT, 128 - CUT, FROM_YP_O, 4)
O_UP = tuple((5, r, CUT // 2, FROM_YM_O, 1) for r in (0, CUT // 2))
O_DOWN = tuple((7, r, CUT // 2, FROM_YP_O, 3) for r in (0, CUT // 2))
S_UP = ((1, 0, CUT, FROM_YM, 1), (1, CUT, 128 - CUT, FROM_YM, 1))
S_DOWN = ((3, 0, CUT, FROM_YP, 3), (3, CUT, 128 - CUT, FROM_YP, 3))
S_ACROSS = ((2, 0, 64, FROM_Y2, 2), (2, 64, 64, FROM_Y2, 2))
X_SUM = ((4, 0, CUT // 2, FROM_X_SUM, 4), (4, CUT // 2, CUT // 2, FROM_X_SUM, 4), (4, CUT, 128 - CUT, FROM_X_SUM, 4))
MESSAGES = X_FIRST + (X_UP, X_DOWN) + O_UP + O_DOWN + S_UP + S_DOWN + S_ACROSS + X_SUM


def device(xl, z, c, xh, y):
    return {"dp": xl * 16 + z * 2 + c, "tensor": xh * 4 + y}


def contract_last(a, b, precision=None):
    return lax.dot_general(
        a, b, (((1,), (1,)), ((), ())), precision=precision, preferred_element_type=jnp.float32
    )


def split(x):
    high = x.astype(jnp.bfloat16)
    return high, (x - high.astype(jnp.float32)).astype(jnp.bfloat16)


def kernel(
    h_hbm, o_hbm, pin_hbm, pout_hbm, out_ref,
    hbuf, obuf, wl, wr, part, recv, fbuf, rows, cols, tiles, tiles_in,
    hsem, osem, wsem, rs_send, rs_recv, row_send, row_recv, col_send, col_recv, t_send, t_recv, line_sem, z_sem, plane_sem,
):
    dp, me = lax.axis_index("dp"), lax.axis_index("tensor")
    xl, z, c = dp // 16, (dp // 2) % 8, dp % 2
    xh, y = me // 4, me % 4
    q = xl * 2 + c
    zpar, zrow = z % 2, z // 2

    def peer(off):
        return lax.rem(xh + off // 4, 2), lax.rem(y + off % 4, 4)

    win = pltpu.make_async_copy(pin_hbm, wl, wsem.at[0])
    wout = pltpu.make_async_copy(pout_hbm, wr, wsem.at[1])

    def load(off):
        a, b = peer(off)
        return (
            pltpu.make_async_copy(h_hbm.at[a * 4 + b], hbuf.at[off], hsem.at[off]),
            pltpu.make_async_copy(o_hbm.at[a * 4 + b], obuf.at[off], osem.at[off]),
        )

    win.start()
    wout.start()
    for off in ORDER[:DEPTH]:
        for copy in load(off):
            copy.start()

    barrier = pltpu.get_barrier_semaphore()

    def greet(dev):
        pl.semaphore_signal(barrier, inc=1, device_id=dev, device_id_type=MESH)

    near = [device(xl, z, c, *peer(off)) for off in (4, 2, 1, 3)]
    near_z = [device(xl, lax.rem(z + dz, NZ), c, xh, y) for dz in (2, 6, 1, 7)]
    others = [device(1 - xl, z, 1 - c, xh, y), device(1 - xl, z, c, xh, y), device(xl, z, 1 - c, xh, y)]
    for dev in near + near_z + others:
        greet(dev)
    greetings = 11

    tiles[...] = jnp.zeros_like(tiles)
    win.wait()
    wout.wait()

    def project(off):
        for copy in load(off):
            copy.wait()
        ahead = ORDER.index(off) + DEPTH
        if ahead < NT:
            for copy in load(ORDER[ahead]):
                copy.start()
        part[off, pl.ds(0, 64)] = contract_last(wl[...], hbuf[off])
        part[off, pl.ds(64, 64)] = contract_last(wr[...], obuf[off])

    def rs_copy(msg):
        chunk, row, count, slot, to = msg
        at = MESSAGES.index(msg)
        return pltpu.make_async_remote_copy(
            src_ref=part.at[chunk, pl.ds(row, count)], dst_ref=recv.at[slot, pl.ds(row, count)],
            send_sem=rs_send.at[at], recv_sem=rs_recv.at[at],
            device_id=device(xl, z, c, *peer(to)), device_id_type=MESH,
        )

    def start(*messages):
        for msg in messages:
            rs_copy(msg).start()

    def arrived(*messages):
        for msg in messages:
            rs_copy(msg).wait_recv()

    for off in (5, 7, 6):
        project(off)
    pl.semaphore_wait(barrier, greetings)
    start(O_UP[0], O_DOWN[0], X_FIRST[0], O_UP[1], O_DOWN[1], X_FIRST[1], X_UP, X_DOWN)
    for dev in near_z:
        pl.semaphore_signal(z_sem, inc=1, device_id=dev, device_id_type=MESH)
    project(1)
    start(S_UP[0])
    project(3)
    start(S_DOWN[0])
    project(4)
    start(X_SUM[2])
    project(2)
    for half in range(2):
        arrived(O_UP[half], O_DOWN[half])
        rowset = pl.ds(CUT // 2 * half, CUT // 2)
        part[4, rowset] += recv[FROM_YM_O, rowset] + recv[FROM_YP_O, rowset]
        start(X_SUM[half])
        arrived(X_FIRST[half])
        rowset = pl.ds(64 * half, 64)
        part[2, rowset] += recv[FROM_X, rowset]
        start(S_ACROSS[half])
        if half == 0:
            for dev in others:
                pl.semaphore_signal(plane_sem, inc=1, device_id=dev, device_id_type=MESH)
    arrived(X_UP, X_DOWN)
    rowset = pl.ds(CUT, 128 - CUT)
    part[1, rowset] += recv[FROM_YM_O, rowset]
    part[3, rowset] += recv[FROM_YP_O, rowset]
    start(S_UP[1], S_DOWN[1])

    pl.semaphore_wait(z_sem, 4)
    pl.semaphore_wait(plane_sem, 3)

    @pl.when(y == zrow)
    def _():
        for t in range(NT):

            pl.semaphore_signal(
                line_sem, inc=1, device_id=device(xh, z, 1 - c, t // 4, t % 4), device_id_type=MESH
            )

            @pl.when((xl != xh) | (me != t))
            def _():
                pl.semaphore_signal(
                    line_sem, inc=1, device_id=device(xh, z, c, t // 4, t % 4), device_id_type=MESH
                )
    project(0)
    arrived(*S_UP, *S_DOWN, *X_SUM, *S_ACROSS)
    total = (part[0] + recv[FROM_YM]) + (recv[FROM_YP] + recv[FROM_X_SUM]) + recv[FROM_Y2]

    scale = 1.0 / math.sqrt(256 * 64)
    right = total[64:]
    gram = contract_last(total[:64], jnp.concatenate([right, right], axis=0), HIGHEST) * scale
    lane = lax.broadcasted_iota(jnp.int32, (32, 128), 1)
    fbuf[...] = jnp.where(lane < 64, gram[:32], gram[32:]).reshape(2, 2, 8, 128)

    def col_copy(to_z, to_xl, to_c):
        return pltpu.make_async_remote_copy(
            src_ref=fbuf.at[to_xl, to_c], dst_ref=cols.at[zpar, me, c],
            send_sem=col_send, recv_sem=col_recv.at[zpar],
            device_id=device(to_xl, to_z, to_c, xl, zrow), device_id_type=MESH,
        )

    def row_copy(off, to_xl, to_c):
        return pltpu.make_async_remote_copy(
            src_ref=fbuf.at[to_xl, to_c], dst_ref=rows.at[xl, me, c],
            send_sem=row_send, recv_sem=row_recv,
            device_id=device(to_xl, z, to_c, *peer(off)), device_id_type=MESH,
        )

    own_line = ((xh == xl) & (y == zrow)).astype(jnp.int32)
    pl.semaphore_wait(line_sem, 4 - own_line)
    for i in range(NZ - 1):
        to_z = jnp.where(i < z, i, i + 1)
        for to_xl in (1 - xl, xl):
            for to_c in (c, 1 - c):
                col_copy(to_z, to_xl, to_c).start()
    for off in range(NT - 1, -1, -1):
        for to_xl in (1 - xl, xl):
            for to_c in (1 - c, c):
                if off or to_xl is not xl or to_c is not c:
                    row_copy(off, to_xl, to_c).start()
    rows[xl, me, c] = fbuf[xl, c]

    row_bytes = rows.reshape(32, 8, 128).at[pl.ds(0, 31)]
    pltpu.make_async_copy(row_bytes, row_bytes, row_recv).wait()
    def wide(ref):
        return jnp.concatenate(
            [jnp.concatenate([ref[a, :, cc, r, :] for a in range(2) for cc in range(2)], axis=0) for r in range(8)],
            axis=1,
        )

    row_high, row_low = split(wide(rows))
    row_split = jnp.concatenate([row_high, row_high, row_low], axis=1)
    for par in range(2):

        @pl.when(2 * y + par != z)
        def _():
            pltpu.make_async_copy(cols.at[par], cols.at[par], col_recv.at[par]).wait()

        @pl.when(2 * y + par == z)
        def _():
            cols[par] = rows[xh]

    col_high, col_low = split(wide(cols))
    acc = contract_last(row_split, jnp.concatenate([col_high, col_low, col_high], axis=1))
    tiles[:, :, pl.ds(0, 32)] = acc.reshape(NQ, 8, 32)

    def t_copy(j):
        p = q ^ j
        return pltpu.make_async_remote_copy(
            src_ref=tiles.at[p], dst_ref=tiles_in.at[q], send_sem=t_send.at[j], recv_sem=t_recv.at[j],
            device_id=device(p // 2, z, p % 2, xh, y), device_id_type=MESH,
        )

    for j in (3, 2, 1):
        t_copy(j).start()
    tiles_in[q] = tiles[q]
    for j in range(1, NQ):
        t_copy(j).wait_recv()
    out_ref[...] = (tiles_in[0] + tiles_in[1] + tiles_in[2] + tiles_in[3])[:, :32]

    for msg in MESSAGES:
        rs_copy(msg).wait_send()
    for j in range(1, NQ):
        t_copy(j).wait_send()
    pltpu.make_async_copy(row_bytes, row_bytes, row_send).wait()
    col_bytes = rows.reshape(32, 8, 128).at[pl.ds(0, 28)]
    pltpu.make_async_copy(col_bytes, col_bytes, col_send).wait()


def per_device(hidden_acts, out_grads, input_basis, output_basis):
    seqs, length, width_ff = hidden_acts.shape
    width_d = out_grads.shape[2]
    f32, bf16 = jnp.float32, jnp.bfloat16
    dma, vmem = pltpu.SemaphoreType.DMA, pltpu.VMEM
    return pl.pallas_call(
        kernel,
        out_shape=jax.ShapeDtypeStruct((8, 32), f32),
        in_specs=[pl.BlockSpec(memory_space=pltpu.HBM)] * 4,
        out_specs=pl.BlockSpec(memory_space=pltpu.VMEM),
        scratch_shapes=[
            vmem((seqs, length, width_ff), bf16),
            vmem((seqs, length, width_d), bf16),
            vmem((64, width_ff), bf16),
            vmem((64, width_d), bf16),
            vmem((NT, 128, length), f32),
            vmem((7, 128, length), f32),
            vmem((2, 2, 8, 128), f32),
            vmem((2, NT, 2, 8, 128), f32),
            vmem((2, NT, 2, 8, 128), f32),
            vmem((NQ, 8, 128), f32),
            vmem((NQ, 8, 128), f32),
            dma((NT,)), dma((NT,)), dma((2,)),
            dma((len(MESSAGES),)), dma((len(MESSAGES),)),
            dma, dma,
            dma, dma((2,)),
            dma((NQ,)), dma((NQ,)),
            pltpu.SemaphoreType.REGULAR, pltpu.SemaphoreType.REGULAR, pltpu.SemaphoreType.REGULAR,
        ],
        compiler_params=pltpu.CompilerParams(
            collective_id=0, has_side_effects=True, vmem_limit_bytes=55168 * 1024
        ),
        cost_estimate=pl.CostEstimate(flops=700_000_000, bytes_accessed=10_000_000, transcendentals=0),
    )(hidden_acts, out_grads, input_basis, output_basis)


def solution(mesh):
    return jax.shard_map(
        per_device,
        mesh=mesh,
        in_specs=(
            P("dp", None, "tensor"),
            P("dp", None, "tensor"),
            P(None, "tensor"),
            P(None, "tensor"),
        ),
        out_specs=P("dp", "tensor"),
        check_vma=False,
    )
```

```python
import math

import jax
import jax.numpy as jnp
from jax import lax
from jax.experimental import pallas as pl
from jax.experimental.pallas import tpu as pltpu
from jax.sharding import PartitionSpec as P

MESH = pl.DeviceIdType.MESH
HIGHEST = lax.Precision.HIGHEST
NT = 8
NQ = 4
NZ = 8
ORDER = (5, 7, 6, 1, 3, 4, 2, 0)
DEPTH = 3
FROM_X, FROM_YM_O, FROM_YP_O, FROM_YM, FROM_YP, FROM_Y2, FROM_X_SUM = range(7)
CUT = 112
X_FIRST = ((6, 64, 64, FROM_X, 4), (6, 0, 64, FROM_X, 4))
X_UP, X_DOWN = (5, CUT, 128 - CUT, FROM_YM_O, 4), (7, CUT, 128 - CUT, FROM_YP_O, 4)
PIECES = ((64, CUT - 64), (0, 64))
O_UP = tuple((5, r, n, FROM_YM_O, 1) for r, n in PIECES)
O_DOWN = tuple((7, r, n, FROM_YP_O, 3) for r, n in PIECES)
S_UP = ((1, 0, CUT, FROM_YM, 1), (1, CUT, 128 - CUT, FROM_YM, 1))
S_DOWN = ((3, 0, CUT, FROM_YP, 3), (3, CUT, 128 - CUT, FROM_YP, 3))
S_ACROSS = ((2, 64, 64, FROM_Y2, 2), (2, 0, 64, FROM_Y2, 2))
X_SUM = tuple((4, r, n, FROM_X_SUM, 4) for r, n in PIECES + ((CUT, 128 - CUT),))
MESSAGES = X_FIRST + (X_UP, X_DOWN) + O_UP + O_DOWN + S_UP + S_DOWN + S_ACROSS + X_SUM


def device(xl, z, c, xh, y):
    return {"dp": xl * 16 + z * 2 + c, "tensor": xh * 4 + y}


def contract_last(a, b, precision=None):
    return lax.dot_general(
        a, b, (((1,), (1,)), ((), ())), precision=precision, preferred_element_type=jnp.float32
    )


def split(x):
    high = x.astype(jnp.bfloat16)
    return high, (x - high.astype(jnp.float32)).astype(jnp.bfloat16)


def kernel(
    h_hbm, o_hbm, pin_hbm, pout_hbm, out_ref,
    hbuf, obuf, wl, wr, part, recv, fbuf, rows, cols, tiles, tiles_in,
    hsem, osem, wsem, rs_send, rs_recv, row_send, row_recv, col_send, col_recv, t_send, t_recv, line_sem, z_sem, plane_sem,
):
    dp, me = lax.axis_index("dp"), lax.axis_index("tensor")
    xl, z, c = dp // 16, (dp // 2) % 8, dp % 2
    xh, y = me // 4, me % 4
    q = xl * 2 + c
    zpar, zrow = z % 2, z // 2

    def peer(off):
        return lax.rem(xh + off // 4, 2), lax.rem(y + off % 4, 4)

    win = pltpu.make_async_copy(pin_hbm, wl, wsem.at[0])
    wout = pltpu.make_async_copy(pout_hbm, wr, wsem.at[1])

    def load_left(off):
        a, b = peer(off)
        return pltpu.make_async_copy(h_hbm.at[a * 4 + b], hbuf.at[off], hsem.at[off])

    def load_right(off):
        a, b = peer(off)
        return pltpu.make_async_copy(o_hbm.at[a * 4 + b], obuf.at[off], osem.at[off])

    wout.start()
    for off in ORDER[:DEPTH]:
        load_right(off).start()
    win.start()
    for off in ORDER[:DEPTH]:
        load_left(off).start()

    barrier = pltpu.get_barrier_semaphore()

    def greet(dev):
        pl.semaphore_signal(barrier, inc=1, device_id=dev, device_id_type=MESH)

    near = [device(xl, z, c, *peer(off)) for off in (4, 2, 1, 3)]
    near_z = [device(xl, lax.rem(z + dz, NZ), c, xh, y) for dz in (2, 6, 1, 7)]
    others = [device(1 - xl, z, 1 - c, xh, y), device(1 - xl, z, c, xh, y), device(xl, z, 1 - c, xh, y)]
    for dev in near + near_z + others:
        greet(dev)
    greetings = 11

    tiles[...] = jnp.zeros_like(tiles)

    def project_left(off):
        load_left(off).wait()
        ahead = ORDER.index(off) + DEPTH
        if ahead < NT:
            load_right(ORDER[ahead]).start()
            load_left(ORDER[ahead]).start()
        part[off, pl.ds(0, 64)] = contract_last(wl[...], hbuf[off])

    def project_right(off):
        load_right(off).wait()
        part[off, pl.ds(64, 64)] = contract_last(wr[...], obuf[off])

    def project(off):
        project_right(off)
        project_left(off)

    def rs_copy(msg):
        chunk, row, count, slot, to = msg
        at = MESSAGES.index(msg)
        return pltpu.make_async_remote_copy(
            src_ref=part.at[chunk, pl.ds(row, count)], dst_ref=recv.at[slot, pl.ds(row, count)],
            send_sem=rs_send.at[at], recv_sem=rs_recv.at[at],
            device_id=device(xl, z, c, *peer(to)), device_id_type=MESH,
        )

    def start(*messages):
        for msg in messages:
            rs_copy(msg).start()

    def arrived(*messages):
        for msg in messages:
            rs_copy(msg).wait_recv()

    wout.wait()
    for off in (5, 7, 6):
        project_right(off)
    win.wait()
    project_left(5)
    pl.semaphore_wait(barrier, greetings)
    start(O_UP[0], O_DOWN[0], X_FIRST[0], X_UP, X_DOWN)
    start(O_UP[1])
    project_left(7)
    start(O_DOWN[1])
    project_left(6)
    start(X_FIRST[1])
    for dev in near_z:
        pl.semaphore_signal(z_sem, inc=1, device_id=dev, device_id_type=MESH)
    project(1)
    start(S_UP[0])
    project(3)
    start(S_DOWN[0])
    project(4)
    start(X_SUM[2])
    project(2)
    for half in range(2):
        arrived(O_UP[half], O_DOWN[half])
        rowset = pl.ds(*PIECES[half])
        part[4, rowset] += recv[FROM_YM_O, rowset] + recv[FROM_YP_O, rowset]
        start(X_SUM[half])
        arrived(X_FIRST[half])
        rowset = pl.ds(64 - 64 * half, 64)
        part[2, rowset] += recv[FROM_X, rowset]
        start(S_ACROSS[half])
        if half == 0:
            for dev in others:
                pl.semaphore_signal(plane_sem, inc=1, device_id=dev, device_id_type=MESH)
    arrived(X_UP, X_DOWN)
    rowset = pl.ds(CUT, 128 - CUT)
    part[1, rowset] += recv[FROM_YM_O, rowset]
    part[3, rowset] += recv[FROM_YP_O, rowset]
    start(S_UP[1], S_DOWN[1])

    pl.semaphore_wait(z_sem, 4)
    pl.semaphore_wait(plane_sem, 3)

    @pl.when(y == zrow)
    def _():
        for t in range(NT):

            pl.semaphore_signal(
                line_sem, inc=1, device_id=device(xh, z, 1 - c, t // 4, t % 4), device_id_type=MESH
            )

            @pl.when((xl != xh) | (me != t))
            def _():
                pl.semaphore_signal(
                    line_sem, inc=1, device_id=device(xh, z, c, t // 4, t % 4), device_id_type=MESH
                )
    project(0)
    arrived(*S_UP, *S_DOWN, *X_SUM, *S_ACROSS)
    total = (part[0] + recv[FROM_YM]) + (recv[FROM_YP] + recv[FROM_X_SUM]) + recv[FROM_Y2]

    scale = 1.0 / math.sqrt(256 * 64)
    right = total[64:]
    gram = contract_last(total[:64], jnp.concatenate([right, right], axis=0), HIGHEST) * scale
    lane = lax.broadcasted_iota(jnp.int32, (32, 128), 1)
    fbuf[...] = jnp.where(lane < 64, gram[:32], gram[32:]).reshape(2, 2, 8, 128)

    def col_copy(to_z, to_xl, to_c):
        return pltpu.make_async_remote_copy(
            src_ref=fbuf.at[to_xl, to_c], dst_ref=cols.at[zpar, me, c],
            send_sem=col_send, recv_sem=col_recv.at[zpar],
            device_id=device(to_xl, to_z, to_c, xl, zrow), device_id_type=MESH,
        )

    def row_copy(off, to_xl, to_c):
        return pltpu.make_async_remote_copy(
            src_ref=fbuf.at[to_xl, to_c], dst_ref=rows.at[xl, me, c],
            send_sem=row_send, recv_sem=row_recv,
            device_id=device(to_xl, z, to_c, *peer(off)), device_id_type=MESH,
        )

    own_line = ((xh == xl) & (y == zrow)).astype(jnp.int32)
    pl.semaphore_wait(line_sem, 4 - own_line)
    for i in range(NZ - 1):
        to_z = jnp.where(i < z, i, i + 1)
        for to_xl in (1 - xl, xl):
            for to_c in (c, 1 - c):
                col_copy(to_z, to_xl, to_c).start()
    for off in range(NT - 1, -1, -1):
        for to_xl in (1 - xl, xl):
            for to_c in (1 - c, c):
                if off or to_xl is not xl or to_c is not c:
                    row_copy(off, to_xl, to_c).start()
    rows[xl, me, c] = fbuf[xl, c]

    row_bytes = rows.reshape(32, 8, 128).at[pl.ds(0, 31)]
    pltpu.make_async_copy(row_bytes, row_bytes, row_recv).wait()
    def wide(ref):
        return jnp.concatenate(
            [jnp.concatenate([ref[a, :, cc, r, :] for a in range(2) for cc in range(2)], axis=0) for r in range(8)],
            axis=1,
        )

    row_high, row_low = split(wide(rows))
    row_split = jnp.concatenate([row_high, row_high, row_low], axis=1)
    for par in range(2):

        @pl.when(2 * y + par != z)
        def _():
            pltpu.make_async_copy(cols.at[par], cols.at[par], col_recv.at[par]).wait()

        @pl.when(2 * y + par == z)
        def _():
            cols[par] = rows[xh]

    col_high, col_low = split(wide(cols))
    acc = contract_last(row_split, jnp.concatenate([col_high, col_low, col_high], axis=1))
    tiles[:, :, pl.ds(0, 32)] = acc.reshape(NQ, 8, 32)

    def t_copy(j):
        p = q ^ j
        return pltpu.make_async_remote_copy(
            src_ref=tiles.at[p], dst_ref=tiles_in.at[q], send_sem=t_send.at[j], recv_sem=t_recv.at[j],
            device_id=device(p // 2, z, p % 2, xh, y), device_id_type=MESH,
        )

    for j in (3, 2, 1):
        t_copy(j).start()
    tiles_in[q] = tiles[q]
    for j in range(1, NQ):
        t_copy(j).wait_recv()
    out_ref[...] = (tiles_in[0] + tiles_in[1] + tiles_in[2] + tiles_in[3])[:, :32]

    for msg in MESSAGES:
        rs_copy(msg).wait_send()
    for j in range(1, NQ):
        t_copy(j).wait_send()
    pltpu.make_async_copy(row_bytes, row_bytes, row_send).wait()
    col_bytes = rows.reshape(32, 8, 128).at[pl.ds(0, 28)]
    pltpu.make_async_copy(col_bytes, col_bytes, col_send).wait()


def per_device(hidden_acts, out_grads, input_basis, output_basis):
    seqs, length, width_ff = hidden_acts.shape
    width_d = out_grads.shape[2]
    f32, bf16 = jnp.float32, jnp.bfloat16
    dma, vmem = pltpu.SemaphoreType.DMA, pltpu.VMEM
    return pl.pallas_call(
        kernel,
        out_shape=jax.ShapeDtypeStruct((8, 32), f32),
        in_specs=[pl.BlockSpec(memory_space=pltpu.HBM)] * 4,
        out_specs=pl.BlockSpec(memory_space=pltpu.VMEM),
        scratch_shapes=[
            vmem((seqs, length, width_ff), bf16),
            vmem((seqs, length, width_d), bf16),
            vmem((64, width_ff), bf16),
            vmem((64, width_d), bf16),
            vmem((NT, 128, length), f32),
            vmem((7, 128, length), f32),
            vmem((2, 2, 8, 128), f32),
            vmem((2, NT, 2, 8, 128), f32),
            vmem((2, NT, 2, 8, 128), f32),
            vmem((NQ, 8, 128), f32),
            vmem((NQ, 8, 128), f32),
            dma((NT,)), dma((NT,)), dma((2,)),
            dma((len(MESSAGES),)), dma((len(MESSAGES),)),
            dma, dma,
            dma, dma((2,)),
            dma((NQ,)), dma((NQ,)),
            pltpu.SemaphoreType.REGULAR, pltpu.SemaphoreType.REGULAR, pltpu.SemaphoreType.REGULAR,
        ],
        compiler_params=pltpu.CompilerParams(
            collective_id=0, has_side_effects=True, vmem_limit_bytes=55168 * 1024
        ),
        cost_estimate=pl.CostEstimate(flops=700_000_000, bytes_accessed=10_000_000, transcendentals=0),
    )(hidden_acts, out_grads, input_basis, output_basis)


def solution(mesh):
    return jax.shard_map(
        per_device,
        mesh=mesh,
        in_specs=(
            P("dp", None, "tensor"),
            P("dp", None, "tensor"),
            P(None, "tensor"),
            P(None, "tensor"),
        ),
        out_specs=P("dp", "tensor"),
        check_vma=False,
    )
```

```python
import math

import jax
import jax.numpy as jnp
from jax import lax
from jax.experimental import pallas as pl
from jax.experimental.pallas import tpu as pltpu
from jax.sharding import PartitionSpec as P

MESH = pl.DeviceIdType.MESH
HIGHEST = lax.Precision.HIGHEST
NT = 8
NQ = 4
NZ = 8
ORDER = (5, 7, 6, 1, 3, 4, 2, 0)
DEPTH = 3
FROM_X, FROM_YM_O, FROM_YP_O, FROM_YM, FROM_YP, FROM_Y2, FROM_X_SUM = range(7)
CUT = 112
X_FIRST = ((6, 64, 64, FROM_X, 4), (6, 0, 64, FROM_X, 4))
X_UP, X_DOWN = (5, CUT, 128 - CUT, FROM_YM_O, 4), (7, CUT, 128 - CUT, FROM_YP_O, 4)
PIECES = ((64, CUT - 64), (0, 64))
O_UP = tuple((5, r, n, FROM_YM_O, 1) for r, n in PIECES)
O_DOWN = tuple((7, r, n, FROM_YP_O, 3) for r, n in PIECES)
S_UP = tuple((1, r, n, FROM_YM, 1) for r, n in PIECES + ((CUT, 128 - CUT),))
S_DOWN = tuple((3, r, n, FROM_YP, 3) for r, n in PIECES + ((CUT, 128 - CUT),))
S_ACROSS = ((2, 64, 64, FROM_Y2, 2), (2, 0, 64, FROM_Y2, 2))
X_SUM = tuple((4, r, n, FROM_X_SUM, 4) for r, n in PIECES + ((CUT, 128 - CUT),))
MESSAGES = X_FIRST + (X_UP, X_DOWN) + O_UP + O_DOWN + S_UP + S_DOWN + S_ACROSS + X_SUM


def device(xl, z, c, xh, y):
    return {"dp": xl * 16 + z * 2 + c, "tensor": xh * 4 + y}


def contract_last(a, b, precision=None):
    return lax.dot_general(
        a, b, (((1,), (1,)), ((), ())), precision=precision, preferred_element_type=jnp.float32
    )


def split(x):
    high = x.astype(jnp.bfloat16)
    return high, (x - high.astype(jnp.float32)).astype(jnp.bfloat16)


def kernel(
    h_hbm, o_hbm, pin_hbm, pout_hbm, out_ref,
    hbuf, obuf, wl, wr, part, recv, fbuf, rows, cols, tiles, tiles_in,
    hsem, osem, wsem, rs_send, rs_recv, row_send, row_recv, col_send, col_recv, t_send, t_recv, line_sem, z_sem, plane_sem,
):
    dp, me = lax.axis_index("dp"), lax.axis_index("tensor")
    xl, z, c = dp // 16, (dp // 2) % 8, dp % 2
    xh, y = me // 4, me % 4
    q = xl * 2 + c
    zpar, zrow = z % 2, z // 2

    def peer(off):
        return lax.rem(xh + off // 4, 2), lax.rem(y + off % 4, 4)

    win = pltpu.make_async_copy(pin_hbm, wl, wsem.at[0])
    wout = pltpu.make_async_copy(pout_hbm, wr, wsem.at[1])

    def load_left(off):
        a, b = peer(off)
        return pltpu.make_async_copy(h_hbm.at[a * 4 + b], hbuf.at[off], hsem.at[off])

    def load_right(off):
        a, b = peer(off)
        return pltpu.make_async_copy(o_hbm.at[a * 4 + b], obuf.at[off], osem.at[off])

    wout.start()
    for off in ORDER[:DEPTH]:
        load_right(off).start()
    win.start()
    for off in ORDER[:DEPTH]:
        load_left(off).start()

    barrier = pltpu.get_barrier_semaphore()

    def greet(dev):
        pl.semaphore_signal(barrier, inc=1, device_id=dev, device_id_type=MESH)

    near = [device(xl, z, c, *peer(off)) for off in (4, 2, 1, 3)]
    near_z = [device(xl, lax.rem(z + dz, NZ), c, xh, y) for dz in (2, 6, 1, 7)]
    others = [device(1 - xl, z, 1 - c, xh, y), device(1 - xl, z, c, xh, y), device(xl, z, 1 - c, xh, y)]
    for dev in near + near_z + others:
        greet(dev)
    greetings = 11

    tiles[...] = jnp.zeros_like(tiles)

    def project_left(off):
        load_left(off).wait()
        ahead = ORDER.index(off) + DEPTH
        if ahead < NT:
            load_right(ORDER[ahead]).start()
            load_left(ORDER[ahead]).start()
        part[off, pl.ds(0, 64)] = contract_last(wl[...], hbuf[off])

    def project_right(off):
        load_right(off).wait()
        part[off, pl.ds(64, 64)] = contract_last(wr[...], obuf[off])

    def project(off):
        project_right(off)
        project_left(off)

    def rs_copy(msg):
        chunk, row, count, slot, to = msg
        at = MESSAGES.index(msg)
        return pltpu.make_async_remote_copy(
            src_ref=part.at[chunk, pl.ds(row, count)], dst_ref=recv.at[slot, pl.ds(row, count)],
            send_sem=rs_send.at[at], recv_sem=rs_recv.at[at],
            device_id=device(xl, z, c, *peer(to)), device_id_type=MESH,
        )

    def start(*messages):
        for msg in messages:
            rs_copy(msg).start()

    def arrived(*messages):
        for msg in messages:
            rs_copy(msg).wait_recv()

    wout.wait()
    for off in (5, 7, 6):
        project_right(off)
    win.wait()
    project_left(5)
    pl.semaphore_wait(barrier, greetings)
    start(O_UP[0], O_DOWN[0], X_FIRST[0], X_UP, X_DOWN)
    start(O_UP[1])
    project_left(7)
    start(O_DOWN[1])
    project_left(6)
    start(X_FIRST[1])
    for dev in near_z:
        pl.semaphore_signal(z_sem, inc=1, device_id=dev, device_id_type=MESH)
    project_right(1)
    start(S_UP[0])
    project_right(3)
    start(S_DOWN[0])
    project_left(1)
    start(S_UP[1])
    project_left(3)
    start(S_DOWN[1])
    project(4)
    start(X_SUM[2])
    project(2)
    for half in range(2):
        arrived(O_UP[half], O_DOWN[half])
        rowset = pl.ds(*PIECES[half])
        part[4, rowset] += recv[FROM_YM_O, rowset] + recv[FROM_YP_O, rowset]
        start(X_SUM[half])
        arrived(X_FIRST[half])
        rowset = pl.ds(64 - 64 * half, 64)
        part[2, rowset] += recv[FROM_X, rowset]
        start(S_ACROSS[half])
        if half == 0:
            for dev in others:
                pl.semaphore_signal(plane_sem, inc=1, device_id=dev, device_id_type=MESH)
    arrived(X_UP, X_DOWN)
    rowset = pl.ds(CUT, 128 - CUT)
    part[1, rowset] += recv[FROM_YM_O, rowset]
    part[3, rowset] += recv[FROM_YP_O, rowset]
    start(S_UP[2], S_DOWN[2])

    pl.semaphore_wait(z_sem, 4)
    pl.semaphore_wait(plane_sem, 3)

    @pl.when(y == zrow)
    def _():
        for t in range(NT):

            pl.semaphore_signal(
                line_sem, inc=1, device_id=device(xh, z, 1 - c, t // 4, t % 4), device_id_type=MESH
            )

            @pl.when((xl != xh) | (me != t))
            def _():
                pl.semaphore_signal(
                    line_sem, inc=1, device_id=device(xh, z, c, t // 4, t % 4), device_id_type=MESH
                )
    project(0)
    arrived(*S_UP, *S_DOWN, *X_SUM, *S_ACROSS)
    total = (part[0] + recv[FROM_YM]) + (recv[FROM_YP] + recv[FROM_X_SUM]) + recv[FROM_Y2]

    scale = 1.0 / math.sqrt(256 * 64)
    right = total[64:]
    gram = contract_last(total[:64], jnp.concatenate([right, right], axis=0), HIGHEST) * scale
    lane = lax.broadcasted_iota(jnp.int32, (32, 128), 1)
    fbuf[...] = jnp.where(lane < 64, gram[:32], gram[32:]).reshape(2, 2, 8, 128)

    def col_copy(to_z, to_xl, to_c):
        return pltpu.make_async_remote_copy(
            src_ref=fbuf.at[to_xl, to_c], dst_ref=cols.at[zpar, me, c],
            send_sem=col_send, recv_sem=col_recv.at[zpar],
            device_id=device(to_xl, to_z, to_c, xl, zrow), device_id_type=MESH,
        )

    def row_copy(off, to_xl, to_c):
        return pltpu.make_async_remote_copy(
            src_ref=fbuf.at[to_xl, to_c], dst_ref=rows.at[xl, me, c],
            send_sem=row_send, recv_sem=row_recv,
            device_id=device(to_xl, z, to_c, *peer(off)), device_id_type=MESH,
        )

    own_line = ((xh == xl) & (y == zrow)).astype(jnp.int32)
    pl.semaphore_wait(line_sem, 4 - own_line)
    for i in range(NZ - 1):
        to_z = jnp.where(i < z, i, i + 1)
        for to_xl in (1 - xl, xl):
            for to_c in (c, 1 - c):
                col_copy(to_z, to_xl, to_c).start()
    for off in range(NT - 1, -1, -1):
        for to_xl in (1 - xl, xl):
            for to_c in (1 - c, c):
                if off or to_xl is not xl or to_c is not c:
                    row_copy(off, to_xl, to_c).start()
    rows[xl, me, c] = fbuf[xl, c]

    row_bytes = rows.reshape(32, 8, 128).at[pl.ds(0, 31)]
    pltpu.make_async_copy(row_bytes, row_bytes, row_recv).wait()
    def wide(ref):
        return jnp.concatenate(
            [jnp.concatenate([ref[a, :, cc, r, :] for a in range(2) for cc in range(2)], axis=0) for r in range(8)],
            axis=1,
        )

    row_high, row_low = split(wide(rows))
    row_split = jnp.concatenate([row_high, row_high, row_low], axis=1)
    for par in range(2):

        @pl.when(2 * y + par != z)
        def _():
            pltpu.make_async_copy(cols.at[par], cols.at[par], col_recv.at[par]).wait()

        @pl.when(2 * y + par == z)
        def _():
            cols[par] = rows[xh]

    col_high, col_low = split(wide(cols))
    acc = contract_last(row_split, jnp.concatenate([col_high, col_low, col_high], axis=1))
    tiles[:, :, pl.ds(0, 32)] = acc.reshape(NQ, 8, 32)

    def t_copy(j):
        p = q ^ j
        return pltpu.make_async_remote_copy(
            src_ref=tiles.at[p], dst_ref=tiles_in.at[q], send_sem=t_send.at[j], recv_sem=t_recv.at[j],
            device_id=device(p // 2, z, p % 2, xh, y), device_id_type=MESH,
        )

    for j in (3, 2, 1):
        t_copy(j).start()
    tiles_in[q] = tiles[q]
    for j in range(1, NQ):
        t_copy(j).wait_recv()
    out_ref[...] = (tiles_in[0] + tiles_in[1] + tiles_in[2] + tiles_in[3])[:, :32]

    for msg in MESSAGES:
        rs_copy(msg).wait_send()
    for j in range(1, NQ):
        t_copy(j).wait_send()
    pltpu.make_async_copy(row_bytes, row_bytes, row_send).wait()
    col_bytes = rows.reshape(32, 8, 128).at[pl.ds(0, 28)]
    pltpu.make_async_copy(col_bytes, col_bytes, col_send).wait()


def per_device(hidden_acts, out_grads, input_basis, output_basis):
    seqs, length, width_ff = hidden_acts.shape
    width_d = out_grads.shape[2]
    f32, bf16 = jnp.float32, jnp.bfloat16
    dma, vmem = pltpu.SemaphoreType.DMA, pltpu.VMEM
    return pl.pallas_call(
        kernel,
        out_shape=jax.ShapeDtypeStruct((8, 32), f32),
        in_specs=[pl.BlockSpec(memory_space=pltpu.HBM)] * 4,
        out_specs=pl.BlockSpec(memory_space=pltpu.VMEM),
        scratch_shapes=[
            vmem((seqs, length, width_ff), bf16),
            vmem((seqs, length, width_d), bf16),
            vmem((64, width_ff), bf16),
            vmem((64, width_d), bf16),
            vmem((NT, 128, length), f32),
            vmem((7, 128, length), f32),
            vmem((2, 2, 8, 128), f32),
            vmem((2, NT, 2, 8, 128), f32),
            vmem((2, NT, 2, 8, 128), f32),
            vmem((NQ, 8, 128), f32),
            vmem((NQ, 8, 128), f32),
            dma((NT,)), dma((NT,)), dma((2,)),
            dma((len(MESSAGES),)), dma((len(MESSAGES),)),
            dma, dma,
            dma, dma((2,)),
            dma((NQ,)), dma((NQ,)),
            pltpu.SemaphoreType.REGULAR, pltpu.SemaphoreType.REGULAR, pltpu.SemaphoreType.REGULAR,
        ],
        compiler_params=pltpu.CompilerParams(
            collective_id=0, has_side_effects=True, vmem_limit_bytes=55168 * 1024
        ),
        cost_estimate=pl.CostEstimate(flops=700_000_000, bytes_accessed=10_000_000, transcendentals=0),
    )(hidden_acts, out_grads, input_basis, output_basis)


def solution(mesh):
    return jax.shard_map(
        per_device,
        mesh=mesh,
        in_specs=(
            P("dp", None, "tensor"),
            P("dp", None, "tensor"),
            P(None, "tensor"),
            P(None, "tensor"),
        ),
        out_specs=P("dp", "tensor"),
        check_vma=False,
    )
```

```python
import math

import jax
import jax.numpy as jnp
from jax import lax
from jax.experimental import pallas as pl
from jax.experimental.pallas import tpu as pltpu
from jax.sharding import PartitionSpec as P

MESH = pl.DeviceIdType.MESH
HIGHEST = lax.Precision.HIGHEST
NT = 8
NQ = 4
NZ = 8
ORDER = (5, 7, 6, 1, 3, 4, 2, 0)
DEPTH = 3
FROM_X, FROM_YM_O, FROM_YP_O, FROM_YM, FROM_YP, FROM_Y2, FROM_X_SUM = range(7)
CUT = 112
X_FIRST = ((6, 64, 64, FROM_X, 4), (6, 0, 64, FROM_X, 4))
X_UP, X_DOWN = (5, CUT, 128 - CUT, FROM_YM_O, 4), (7, CUT, 128 - CUT, FROM_YP_O, 4)
PIECES = ((64, CUT - 64), (0, 64))
O_UP = tuple((5, r, n, FROM_YM_O, 1) for r, n in PIECES)
O_DOWN = tuple((7, r, n, FROM_YP_O, 3) for r, n in PIECES)
S_UP = tuple((1, r, n, FROM_YM, 1) for r, n in PIECES + ((CUT, 128 - CUT),))
S_DOWN = tuple((3, r, n, FROM_YP, 3) for r, n in PIECES + ((CUT, 128 - CUT),))
S_ACROSS = ((2, 64, 64, FROM_Y2, 2), (2, 0, 64, FROM_Y2, 2))
X_SUM = tuple((4, r, n, FROM_X_SUM, 4) for r, n in PIECES + ((CUT, 128 - CUT),))
MESSAGES = X_FIRST + (X_UP, X_DOWN) + O_UP + O_DOWN + S_UP + S_DOWN + S_ACROSS + X_SUM


def device(xl, z, c, xh, y):
    return {"dp": xl * 16 + z * 2 + c, "tensor": xh * 4 + y}


def contract_last(a, b, precision=None):
    return lax.dot_general(
        a, b, (((1,), (1,)), ((), ())), precision=precision, preferred_element_type=jnp.float32
    )


def split(x):
    high = x.astype(jnp.bfloat16)
    return high, (x - high.astype(jnp.float32)).astype(jnp.bfloat16)


def kernel(
    h_hbm, o_hbm, pin_hbm, pout_hbm, out_ref,
    hbuf, obuf, wl, wr, part, recv, fbuf, rows, cols, tiles, tiles_in,
    hsem, osem, wsem, rs_send, rs_recv, row_send, row_recv, col_send, col_recv, t_send, t_recv, line_sem, z_sem, plane_sem,
):
    dp, me = lax.axis_index("dp"), lax.axis_index("tensor")
    xl, z, c = dp // 16, (dp // 2) % 8, dp % 2
    xh, y = me // 4, me % 4
    q = xl * 2 + c
    zpar, zrow = z % 2, z // 2

    def peer(off):
        return lax.rem(xh + off // 4, 2), lax.rem(y + off % 4, 4)

    win = pltpu.make_async_copy(pin_hbm, wl, wsem.at[0])
    wout = pltpu.make_async_copy(pout_hbm, wr, wsem.at[1])

    def load_left(off):
        a, b = peer(off)
        return pltpu.make_async_copy(h_hbm.at[a * 4 + b], hbuf.at[off], hsem.at[off])

    def load_right(off):
        a, b = peer(off)
        return pltpu.make_async_copy(o_hbm.at[a * 4 + b], obuf.at[off], osem.at[off])

    wout.start()
    for off in ORDER[:DEPTH]:
        load_right(off).start()
    win.start()
    for off in ORDER[:DEPTH]:
        load_left(off).start()

    barrier = pltpu.get_barrier_semaphore()

    def greet(dev):
        pl.semaphore_signal(barrier, inc=1, device_id=dev, device_id_type=MESH)

    near = [device(xl, z, c, *peer(off)) for off in (4, 2, 1, 3)]
    near_z = [device(xl, lax.rem(z + dz, NZ), c, xh, y) for dz in (2, 6, 1, 7)]
    others = [device(1 - xl, z, 1 - c, xh, y), device(1 - xl, z, c, xh, y), device(xl, z, 1 - c, xh, y)]
    for dev in near + near_z + others:
        greet(dev)
    greetings = 11

    tiles[...] = jnp.zeros_like(tiles)

    def project_left(off):
        load_left(off).wait()
        ahead = ORDER.index(off) + DEPTH
        if ahead < NT:
            load_right(ORDER[ahead]).start()
            load_left(ORDER[ahead]).start()
        part[off, pl.ds(0, 64)] = contract_last(wl[...], hbuf[off])

    def project_right(off):
        load_right(off).wait()
        part[off, pl.ds(64, 64)] = contract_last(wr[...], obuf[off])

    def project(off):
        project_right(off)
        project_left(off)

    def rs_copy(msg):
        chunk, row, count, slot, to = msg
        at = MESSAGES.index(msg)
        return pltpu.make_async_remote_copy(
            src_ref=part.at[chunk, pl.ds(row, count)], dst_ref=recv.at[slot, pl.ds(row, count)],
            send_sem=rs_send.at[at], recv_sem=rs_recv.at[at],
            device_id=device(xl, z, c, *peer(to)), device_id_type=MESH,
        )

    def start(*messages):
        for msg in messages:
            rs_copy(msg).start()

    def arrived(*messages):
        for msg in messages:
            rs_copy(msg).wait_recv()

    wout.wait()
    for off in (5, 7, 6):
        project_right(off)
    win.wait()
    project_left(5)
    pl.semaphore_wait(barrier, greetings)
    start(O_UP[0], O_DOWN[0], X_FIRST[0], X_UP, X_DOWN)
    start(O_UP[1])
    project_left(7)
    start(O_DOWN[1])
    project_left(6)
    start(X_FIRST[1])
    for dev in near_z:
        pl.semaphore_signal(z_sem, inc=1, device_id=dev, device_id_type=MESH)
    project_right(1)
    start(S_UP[0])
    project_right(3)
    start(S_DOWN[0])
    project_left(1)
    start(S_UP[1])
    project_left(3)
    start(S_DOWN[1])
    project(4)
    start(X_SUM[2])
    project(2)
    for half in range(2):
        arrived(X_FIRST[half])
        rowset = pl.ds(64 - 64 * half, 64)
        part[2, rowset] += recv[FROM_X, rowset]
        start(S_ACROSS[half])
        arrived(O_UP[half], O_DOWN[half])
        rowset = pl.ds(*PIECES[half])
        part[4, rowset] += recv[FROM_YM_O, rowset] + recv[FROM_YP_O, rowset]
        start(X_SUM[half])
        if half == 0:
            for dev in others:
                pl.semaphore_signal(plane_sem, inc=1, device_id=dev, device_id_type=MESH)
    arrived(X_UP, X_DOWN)
    rowset = pl.ds(CUT, 128 - CUT)
    part[1, rowset] += recv[FROM_YM_O, rowset]
    part[3, rowset] += recv[FROM_YP_O, rowset]
    start(S_UP[2], S_DOWN[2])

    pl.semaphore_wait(z_sem, 4)
    pl.semaphore_wait(plane_sem, 3)

    @pl.when(y == zrow)
    def _():
        for t in range(NT):

            pl.semaphore_signal(
                line_sem, inc=1, device_id=device(xh, z, 1 - c, t // 4, t % 4), device_id_type=MESH
            )

            @pl.when((xl != xh) | (me != t))
            def _():
                pl.semaphore_signal(
                    line_sem, inc=1, device_id=device(xh, z, c, t // 4, t % 4), device_id_type=MESH
                )
    project(0)
    arrived(*S_UP, *S_DOWN, *X_SUM, *S_ACROSS)
    total = (part[0] + recv[FROM_YM]) + (recv[FROM_YP] + recv[FROM_X_SUM]) + recv[FROM_Y2]

    scale = 1.0 / math.sqrt(256 * 64)
    right = total[64:]
    gram = contract_last(total[:64], jnp.concatenate([right, right], axis=0), HIGHEST) * scale
    lane = lax.broadcasted_iota(jnp.int32, (32, 128), 1)
    fbuf[...] = jnp.where(lane < 64, gram[:32], gram[32:]).reshape(2, 2, 8, 128)

    def col_copy(to_z, to_xl, to_c):
        return pltpu.make_async_remote_copy(
            src_ref=fbuf.at[to_xl, to_c], dst_ref=cols.at[zpar, me, c],
            send_sem=col_send, recv_sem=col_recv.at[zpar],
            device_id=device(to_xl, to_z, to_c, xl, zrow), device_id_type=MESH,
        )

    def row_copy(off, to_xl, to_c):
        return pltpu.make_async_remote_copy(
            src_ref=fbuf.at[to_xl, to_c], dst_ref=rows.at[xl, me, c],
            send_sem=row_send, recv_sem=row_recv,
            device_id=device(to_xl, z, to_c, *peer(off)), device_id_type=MESH,
        )

    own_line = ((xh == xl) & (y == zrow)).astype(jnp.int32)
    pl.semaphore_wait(line_sem, 4 - own_line)
    for i in range(NZ - 1):
        to_z = jnp.where(i < z, i, i + 1)
        for to_xl in (1 - xl, xl):
            for to_c in (c, 1 - c):
                col_copy(to_z, to_xl, to_c).start()
    for off in range(NT - 1, -1, -1):
        for to_xl in (1 - xl, xl):
            for to_c in (1 - c, c):
                if off or to_xl is not xl or to_c is not c:
                    row_copy(off, to_xl, to_c).start()
    rows[xl, me, c] = fbuf[xl, c]

    row_bytes = rows.reshape(32, 8, 128).at[pl.ds(0, 31)]
    pltpu.make_async_copy(row_bytes, row_bytes, row_recv).wait()
    def wide(ref):
        return jnp.concatenate(
            [jnp.concatenate([ref[a, :, cc, r, :] for a in range(2) for cc in range(2)], axis=0) for r in range(8)],
            axis=1,
        )

    row_high, row_low = split(wide(rows))
    row_split = jnp.concatenate([row_high, row_high, row_low], axis=1)
    for par in range(2):

        @pl.when(2 * y + par != z)
        def _():
            pltpu.make_async_copy(cols.at[par], cols.at[par], col_recv.at[par]).wait()

        @pl.when(2 * y + par == z)
        def _():
            cols[par] = rows[xh]

    col_high, col_low = split(wide(cols))
    acc = contract_last(row_split, jnp.concatenate([col_high, col_low, col_high], axis=1))
    tiles[:, :, pl.ds(0, 32)] = acc.reshape(NQ, 8, 32)

    def t_copy(j):
        p = q ^ j
        return pltpu.make_async_remote_copy(
            src_ref=tiles.at[p], dst_ref=tiles_in.at[q], send_sem=t_send.at[j], recv_sem=t_recv.at[j],
            device_id=device(p // 2, z, p % 2, xh, y), device_id_type=MESH,
        )

    for j in (3, 2, 1):
        t_copy(j).start()
    tiles_in[q] = tiles[q]
    for j in range(1, NQ):
        t_copy(j).wait_recv()
    out_ref[...] = (tiles_in[0] + tiles_in[1] + tiles_in[2] + tiles_in[3])[:, :32]

    for msg in MESSAGES:
        rs_copy(msg).wait_send()
    for j in range(1, NQ):
        t_copy(j).wait_send()
    pltpu.make_async_copy(row_bytes, row_bytes, row_send).wait()
    col_bytes = rows.reshape(32, 8, 128).at[pl.ds(0, 28)]
    pltpu.make_async_copy(col_bytes, col_bytes, col_send).wait()


def per_device(hidden_acts, out_grads, input_basis, output_basis):
    seqs, length, width_ff = hidden_acts.shape
    width_d = out_grads.shape[2]
    f32, bf16 = jnp.float32, jnp.bfloat16
    dma, vmem = pltpu.SemaphoreType.DMA, pltpu.VMEM
    return pl.pallas_call(
        kernel,
        out_shape=jax.ShapeDtypeStruct((8, 32), f32),
        in_specs=[pl.BlockSpec(memory_space=pltpu.HBM)] * 4,
        out_specs=pl.BlockSpec(memory_space=pltpu.VMEM),
        scratch_shapes=[
            vmem((seqs, length, width_ff), bf16),
            vmem((seqs, length, width_d), bf16),
            vmem((64, width_ff), bf16),
            vmem((64, width_d), bf16),
            vmem((NT, 128, length), f32),
            vmem((7, 128, length), f32),
            vmem((2, 2, 8, 128), f32),
            vmem((2, NT, 2, 8, 128), f32),
            vmem((2, NT, 2, 8, 128), f32),
            vmem((NQ, 8, 128), f32),
            vmem((NQ, 8, 128), f32),
            dma((NT,)), dma((NT,)), dma((2,)),
            dma((len(MESSAGES),)), dma((len(MESSAGES),)),
            dma, dma,
            dma, dma((2,)),
            dma((NQ,)), dma((NQ,)),
            pltpu.SemaphoreType.REGULAR, pltpu.SemaphoreType.REGULAR, pltpu.SemaphoreType.REGULAR,
        ],
        compiler_params=pltpu.CompilerParams(
            collective_id=0, has_side_effects=True, vmem_limit_bytes=55168 * 1024
        ),
        cost_estimate=pl.CostEstimate(flops=700_000_000, bytes_accessed=10_000_000, transcendentals=0),
    )(hidden_acts, out_grads, input_basis, output_basis)


def solution(mesh):
    return jax.shard_map(
        per_device,
        mesh=mesh,
        in_specs=(
            P("dp", None, "tensor"),
            P("dp", None, "tensor"),
            P(None, "tensor"),
            P(None, "tensor"),
        ),
        out_specs=P("dp", "tensor"),
        check_vma=False,
    )
```
